512 devices in a mesh: dp: 32 (over z_lo, y), tensor: 16 (over z_hi, x, core).
Axes of the slice: x: 4, y: 4, z: 16 (z_hi: 2, z_lo: 8; z = z_hi * 8 + z_lo), core: 2. Of those that a mesh axis runs over, the one named last changes fastest.
Arguments:
- hidden: bfloat16 [8192, 8192], P('dp'), may hold values from -6 to 6
- norm_gain: float32 [8192], replicated, may hold values from 0.1 to 1.9
- w_query: bfloat16 [8192, 4096], P('dp', 'tensor'), may hold values from -0.0447466 to 0.0447466
- w_key: bfloat16 [8192, 512], P('dp', 'tensor'), may hold values from -0.0447466 to 0.0447466
- w_value: bfloat16 [8192, 512], P('dp', 'tensor'), may hold values from -0.0625 to 0.0625
- grad_context: bfloat16 [8192, 4096], P('dp', 'tensor'), may hold values from -6 to 6
Outputs:
- grad_hidden: bfloat16 [8192, 8192], P(('dp', 'tensor'))
The draws below stay inside these ranges and needn't reach their ends.
All inputs are finite; a program needn't handle non-finite values.
Results may differ from the reference program's by a relative error of at most 0.023.
Values may be sent and summed in bfloat16 or wider, within the bound.
A program may use at most 64 MiB of HBM per device.

```python
import math
import jax
import jax.numpy as jnp
from jax import lax

D = 8192
HQ = 32
KVH = 4
HD = 128
SEQ = 256
TOKENS = 8192
N_DP = 32
N_TENSOR = 16


def draw_w_query(key, part):
    own_key = jax.random.fold_in(key, 5)
    drawn = jax.random.truncated_normal(own_key, -4.0, 4.0, (D, HQ, HD), jnp.float32)
    return (jnp.clip(drawn, -4.0, 4.0).reshape(D, HQ * HD) * D ** (-0.5)).astype(jnp.bfloat16)


def draw_w_key(key, part):
    own_key = jax.random.fold_in(key, 7)
    drawn = jax.random.truncated_normal(own_key, -4.0, 4.0, (D, KVH, HD), jnp.float32)
    return (jnp.clip(drawn, -4.0, 4.0).reshape(D, KVH * HD) * D ** (-0.5)).astype(jnp.bfloat16)


def draw_hidden(key, part):
    own_key = jax.random.fold_in(key, 3)
    seq_count = TOKENS // SEQ
    drawn = jax.random.truncated_normal(jax.random.fold_in(own_key, 1), -6.0, 6.0, (seq_count, SEQ, D), jnp.float32)
    return drawn.reshape(TOKENS, D).astype(jnp.bfloat16)


def block_scale(stream_key, shape, split, least, top_value):
    loudness, own = 1.0, jax.random.fold_in(stream_key, 6)
    for position, shards_of in split:
        draws = jnp.exp(jax.random.uniform(jax.random.fold_in(own, position), (shards_of,), jnp.float32, least / len(split), top_value / len(split)))
        loudness = loudness * jnp.repeat(draws, shape[position] // shards_of).reshape([-1 if axis == position else 1 for axis in range(len(shape))])
    return loudness


def gaussian(key, extent, scale, most, split=(), kind=jnp.bfloat16):
    gain = block_scale(key, extent, split, -0.22, 0.18) if split else 1.0
    entries = jax.random.normal(key, extent, jnp.float32) * scale * gain
    return jnp.minimum(jnp.maximum(entries, -most), most).astype(kind)


def setup_inputs(seed: int = 0) -> dict:
    keys = jax.random.split(jax.random.key(seed), 7)
    hidden = draw_hidden(jax.random.fold_in(keys[6], 71), 0)
    norm_gain = jnp.clip(1.0 + 0.18 * jax.random.normal(keys[1], (D,), jnp.float32), 0.1, 1.9)
    w_query = draw_w_query(jax.random.fold_in(keys[6], 71), 0)
    w_key = draw_w_key(jax.random.fold_in(keys[6], 71), 0)
    w_value = gaussian(keys[4], (D, KVH * HD), D ** -0.5, 0.0625, ((0, 32), (1, 16)))
    grad_context = gaussian(keys[5], (TOKENS, HQ * HD), 1.0, 6.0, ((0, 32), (1, 16)))
    return {"hidden": hidden, "norm_gain": norm_gain, "w_query": w_query, "w_key": w_key, "w_value": w_value, "grad_context": grad_context}


rope_theta = 500000.0

def rotate(values, col_start, direction):
    row_count = values.shape[0]
    col_count = values.shape[1]
    paired = values.reshape(row_count, col_count // 2, 2)
    even_part = paired[:, :, 0]
    odd_part = paired[:, :, 1]
    columns = col_start + 2 * jnp.arange(col_count // 2, dtype=jnp.int32)
    pair_index = (columns % HD // 2).astype(jnp.float32)
    frequency = jnp.exp(pair_index * (-2.0 * math.log(rope_theta) / HD))
    angles = jnp.arange(row_count, dtype=jnp.int32).astype(jnp.float32)[:, None] * frequency[None, :]
    cosine = jnp.cos(angles)
    sine_part = direction * jnp.sin(angles)
    return jnp.stack([even_part * cosine - odd_part * sine_part, even_part * sine_part + odd_part * cosine], -1).reshape(row_count, col_count)

def one_sequence(hidden, grad_context, norm_gain, w_query, w_key, w_value):
    hidden_f = hidden.astype(jnp.float32)
    inverse = lax.rsqrt(lax.optimization_barrier(jnp.mean(hidden_f * hidden_f, axis=1, keepdims=True)) + 1e-05)
    normed = (hidden_f * inverse * norm_gain).astype(jnp.bfloat16)
    query_b = rotate(jnp.dot(normed, w_query, preferred_element_type=jnp.float32), 0, 1.0).astype(jnp.bfloat16)
    key_b = rotate(jnp.dot(normed, w_key, preferred_element_type=jnp.float32), 0, 1.0).astype(jnp.bfloat16)
    value_b = jnp.dot(normed, w_value, preferred_element_type=jnp.float32).astype(jnp.bfloat16)
    group_size = HQ // KVH
    query_heads = query_b.astype(jnp.float32).reshape(SEQ, HQ, HD)
    key_heads = jnp.repeat(key_b.astype(jnp.float32).reshape(SEQ, KVH, HD), group_size, axis=1)
    value_heads = jnp.repeat(value_b.astype(jnp.float32).reshape(SEQ, KVH, HD), group_size, axis=1)
    grad_heads = grad_context.astype(jnp.float32).reshape(SEQ, HQ, HD)
    scale = 1.0 / math.sqrt(HD)
    scores = jnp.einsum('qhd,khd->hqk', query_heads, key_heads) * scale
    positions = jnp.arange(SEQ, dtype=jnp.int32)
    causal = positions[:, None] >= positions[None, :]
    scores = jnp.where(causal[None], scores, jnp.float32(-1e+30))
    peak = lax.optimization_barrier(jnp.max(scores, axis=-1, keepdims=True))
    weights = jnp.exp(scores - peak)
    probs = weights / lax.optimization_barrier(jnp.sum(weights, axis=-1, keepdims=True))
    probs_b = probs.astype(jnp.bfloat16)
    grad_probs = jnp.einsum('qhd,khd->hqk', grad_heads, value_heads)
    delta = lax.optimization_barrier(jnp.sum(probs * grad_probs, axis=-1, keepdims=True))
    grad_scores = (probs * (grad_probs - delta) * scale).astype(jnp.bfloat16).astype(jnp.float32)
    grad_query = jnp.einsum('hqk,khd->qhd', grad_scores, key_heads).reshape(SEQ, HQ * HD)
    grad_query_b = rotate(grad_query, 0, -1.0).astype(jnp.bfloat16)
    grad_key = jnp.einsum('hqk,qhd->khd', grad_scores, query_heads).reshape(SEQ, KVH, group_size, HD).sum(2)
    grad_key_b = rotate(grad_key.reshape(SEQ, KVH * HD), 0, -1.0).astype(jnp.bfloat16)
    grad_value = jnp.einsum('hqk,qhd->khd', probs_b.astype(jnp.float32), grad_heads).reshape(SEQ, KVH, group_size, HD).sum(2)
    grad_value_b = grad_value.reshape(SEQ, KVH * HD).astype(jnp.bfloat16)
    query_block = HQ * HD // N_TENSOR
    key_block = KVH * HD // N_TENSOR
    grad_normed = jnp.zeros((SEQ, D), jnp.float32)
    for block_index in range(N_TENSOR):
        q_lo = block_index * query_block
        k_lo = block_index * key_block
        term = jnp.dot(grad_query_b[:, q_lo:q_lo + query_block], w_query[:, q_lo:q_lo + query_block].T, preferred_element_type=jnp.float32)
        term = term + jnp.dot(grad_key_b[:, k_lo:k_lo + key_block], w_key[:, k_lo:k_lo + key_block].T, preferred_element_type=jnp.float32)
        term = term + jnp.dot(grad_value_b[:, k_lo:k_lo + key_block], w_value[:, k_lo:k_lo + key_block].T, preferred_element_type=jnp.float32)
        grad_normed = grad_normed + term.astype(jnp.bfloat16).astype(jnp.float32)
    scaled = grad_normed * norm_gain
    mean_term = lax.optimization_barrier(jnp.mean(scaled * hidden_f, axis=1, keepdims=True))
    result = inverse * (scaled - hidden_f * inverse * inverse * mean_term)
    return result.astype(jnp.bfloat16)

def reference(hidden, norm_gain, w_query, w_key, w_value, grad_context):
    stacked_hidden = hidden.reshape(N_DP, SEQ, D)
    stacked_grad = grad_context.reshape(N_DP, SEQ, HQ * HD)

    def apply_one(pair_items):
        return one_sequence(pair_items[0], pair_items[1], norm_gain, w_query, w_key, w_value)
    outputs = lax.map(apply_one, (stacked_hidden, stacked_grad))
    return outputs.reshape(N_DP * SEQ, D)
```

```python
import functools
import math

import jax
import jax.numpy as jnp
import numpy as np
from jax import lax
from jax.experimental import pallas as pl
from jax.experimental.pallas import tpu as pltpu
from jax.sharding import PartitionSpec as P

D = 8192
HD = 128
SEQ = 256
NZ, NY, NX = 8, 4, 4
SLOTS = NZ * NY
ROWS = 640
HALF = ROWS // 2
ROPE_THETA = 500000.0
SCALE = 1.0 / math.sqrt(HD)
MESH = pl.DeviceIdType.MESH
F32, BF16 = jnp.float32, jnp.bfloat16


def rotary_tables():
    lane = np.arange(HD)
    frequency = np.exp((lane // 2) * (-2.0 * math.log(ROPE_THETA) / HD))
    angle = np.arange(SEQ)[:, None] * frequency[None, :]
    cosine = np.cos(angle)
    sine = np.sin(angle) * np.where(lane % 2 == 0, -1.0, 1.0)[None, :]
    packed_cos = np.ones((4, 128, 128))
    packed_sin = np.zeros((4, 128, 128))
    for rank in range(4):
        columns = slice(32 * rank, 32 * rank + 32)
        for part in range(2):
            rows = slice(128 * part, 128 * part + 128)
            packed_cos[rank, :, 64 * part : 64 * part + 32] = cosine[rows, columns]
            packed_sin[rank, :, 64 * part : 64 * part + 32] = sine[rows, columns]
    return [table.astype(np.float32) for table in (cosine, sine, packed_cos, packed_sin)]


def dot(left, right):
    return lax.dot_general(left, right, (((1,), (0,)), ((), ())), preferred_element_type=F32)


def dot_rows(left, right):
    return lax.dot_general(left, right, (((1,), (1,)), ((), ())), preferred_element_type=F32)


def dot_columns(left, right):
    return lax.dot_general(left, right, (((0,), (0,)), ((), ())), preferred_element_type=F32)


def lanes_of(value):
    return lax.broadcasted_iota(jnp.int32, value.shape, 1)


def rotate(value, cosine, sine):
    left = pltpu.roll(value, 127, 1)
    right = pltpu.roll(value, 1, 1)
    swapped = jnp.where(lanes_of(value) % 2 == 0, left, right)
    return value * cosine + swapped * sine


def kernel(
    hid_ref, gain_ref, wq_ref, wk_ref, wv_ref, gc_ref, cos_ref, sin_ref, kcos_ref, ksin_ref,
    out_ref,
    hid, W, N, qacc, kvacc, kvs, dks, dkr, A,
    sibs, sibr, own, S, xrelay, xin, fs, zsend, zin, G,
    hid_sem, load_sem, ag_recv, ag_send, kv_recv, kv_send, dk_recv, dk_send,
    sib_recv, sib_send, x_recv, x_send, z_recv, z_send,
):
    dp = lax.axis_index("dp")
    tensor = lax.axis_index("tensor")
    z, y = dp // NY, dp % NY
    zh, x, c = tensor // 8, (tensor // 2) % NX, tensor % 2
    rank = tensor % 4
    yl, yr, yo = (y + 3) % 4, (y + 1) % 4, (y + 2) % 4
    xl, xr, xo = (x + 3) % 4, (x + 1) % 4, (x + 2) % 4

    def at_dp(zz, yy):
        return (zz * NY + yy, tensor)

    def at_tensor(zhh, xx, cc):
        return (dp, zhh * 8 + xx * 2 + cc)

    up, down = at_dp(z + 1, y), at_dp(z - 1, y)
    to_yl, to_yr = at_dp(z, yl), at_dp(z, yr)
    to_xl, to_xr = at_tensor(zh, xl, c), at_tensor(zh, xr, c)
    sibling = at_tensor(zh, x, 1 - c)
    far = at_tensor(1 - zh, x, c)
    x_pair = x + 1 - 2 * (x % 2)
    group = {1: sibling, 2: at_tensor(zh, x_pair, c), 3: at_tensor(zh, x_pair, 1 - c)}

    def remote(src, dst, send, recv, device):
        return pltpu.make_async_remote_copy(
            src_ref=src, dst_ref=dst, send_sem=send, recv_sem=recv, device_id=device, device_id_type=MESH
        )

    mine = z * NY + y
    load_q0 = pltpu.make_async_copy(wq_ref.at[:, pl.ds(0, 128)], W.at[mine, pl.ds(0, 256)], load_sem.at[0])
    load_q1 = pltpu.make_async_copy(wq_ref.at[:, pl.ds(128, 128)], W.at[mine, pl.ds(256, 256)], load_sem.at[1])
    load_hid = pltpu.make_async_copy(hid_ref, hid, hid_sem)
    load_q0.start()
    load_q1.start()
    barrier = pltpu.get_barrier_semaphore()

    def greet(device):
        pl.semaphore_signal(barrier, inc=1, device_id=device, device_id_type=MESH)

    for device in (to_yl, to_yr, to_xl, to_xr, sibling, group[3], far):
        greet(device)

    @pl.when(z < NZ - 1)
    def _():
        greet(up)

    @pl.when(z > 0)
    def _():
        greet(down)

    load_hid.start()
    wk, wv = wk_ref[...].astype(F32), wv_ref[...].astype(F32)
    packed = jnp.concatenate([wk[:128], wv[:128], wk[128:], wv[128:]], axis=1)
    W[mine, 512:640, :] = packed.astype(BF16)
    load_q0.wait()
    load_q1.wait()
    pl.semaphore_wait(barrier, 7 + jnp.where(z < NZ - 1, 1, 0) + jnp.where(z > 0, 1, 0))

    def block(i, device, kind):
        return remote(W.at[i], W.at[i], ag_send.at[kind, i], ag_recv.at[i, 0], device)

    def half_block(i, part, device):
        rows = pl.ds(part * HALF, HALF)
        return remote(W.at[i, rows], W.at[i, rows], ag_send.at[3, i], ag_recv.at[i, part], device)

    def plane(n):
        s = (n + 1) // 2
        return jnp.where(n % 2 == 1, z - s, z + s)

    def inside(j):
        return jnp.logical_and(j >= 0, j < NZ)

    def go_up(j):
        return jnp.logical_and(j <= z, z < NZ - 1)

    def go_down(j):
        return jnp.logical_and(j >= z, z > 0)

    def spread(j):
        i = j * NY + y

        @pl.when(go_up(j))
        def _():
            block(i, up, 0).start()

        @pl.when(go_down(j))
        def _():
            block(i, down, 4).start()

        block(i, to_yr, 1).start()
        block(i, to_yl, 2).start()

    def multiply(i):
        columns = pl.ds(pl.multiple_of(i * 256, 256), 256)
        rows = N[:, columns]
        qacc[0] += dot(rows, W[i, 0:256, :])
        qacc[1] += dot(rows, W[i, 256:512, :])
        both = W[i, 512:640, :]
        kvacc[0] += dot(rows[:, 0:128], both)
        kvacc[1] += dot(rows[:, 128:256], both)

    spread(z)
    qacc[...] = jnp.zeros_like(qacc)
    kvacc[...] = jnp.zeros_like(kvacc)
    load_hid.wait()

    def norm_rows(b, carry):
        rows = pl.ds(pl.multiple_of(b * 16, 16), 16)
        values = hid[rows, :].astype(F32)
        inverse = lax.rsqrt(jnp.mean(values * values, axis=1, keepdims=True) + 1e-05)
        N[rows, :] = (values * inverse * gain_ref[...]).astype(BF16)
        return carry

    lax.fori_loop(0, SEQ // 16, norm_rows, 0)

    def gather_step(n, carry):
        ja = plane(n)

        @pl.when(jnp.logical_and(inside(ja), jnp.logical_and(n > 0, n < 15)))
        def _():
            i = ja * NY + y
            block(i, up, 0).wait_recv()
            spread(ja)

        jb = plane(n - 2)

        @pl.when(jnp.logical_and(inside(jb), jnp.logical_and(n >= 2, n < 17)))
        def _():
            i_left, i_right = jb * NY + yl, jb * NY + yr
            block(i_left, to_yr, 1).wait_recv()
            half_block(i_left, 0, to_yr).start()
            block(i_right, to_yl, 2).wait_recv()
            half_block(i_right, 1, to_yl).start()
            multiply(jb * NY + y)
            multiply(i_left)
            multiply(i_right)

        jc = plane(n - 4)

        @pl.when(jnp.logical_and(inside(jc), n >= 4))
        def _():
            i = jc * NY + yo
            half_block(i, 0, to_yr).wait_recv()
            half_block(i, 1, to_yl).wait_recv()
            multiply(i)

        return carry

    lax.fori_loop(0, 19, gather_step, 0)

    lane = lax.broadcasted_iota(jnp.int32, (128, 128), 1)
    kva, kvb = kvacc[0], kvacc[1]
    low = kva[:128] + pltpu.roll(kvb[:128], 64, 1)
    high = pltpu.roll(kva[128:], 64, 1) + kvb[128:]
    kv_own = rotate(jnp.where(lane < 64, low, high), kcos_ref[rank], ksin_ref[rank])
    kvs[rank] = kv_own.astype(BF16)

    def peer(step):
        if step == 1:
            return rank + 1 - 2 * (rank % 2)
        if step == 2:
            return (rank + 2) % 4
        return 3 - rank

    def kv_copy(step):
        return remote(kvs.at[rank], kvs.at[rank], kv_send.at[step - 1], kv_recv.at[step - 1], group[step])

    for step in (1, 2, 3):
        kv_copy(step).start()
    q_heads = []
    for h in range(2):
        q_heads.append(rotate(qacc[h], cos_ref[...], sin_ref[...]).astype(BF16))
    for step in (1, 2, 3):
        kv_copy(step).wait()

    def unpack(shift):
        parts = []
        for part in range(2):
            total = jnp.zeros((128, 128), F32)
            for r in range(4):
                piece = kvs[r].astype(F32)
                amount = (32 * r - shift - 64 * part) % 128
                piece = pltpu.roll(piece, amount, 1) if amount else piece
                total = jnp.where(lane // 32 == r, piece, total)
            parts.append(total)
        return jnp.concatenate(parts, axis=0).astype(BF16)

    k_head, v_head = unpack(0), unpack(32)
    row_id = lax.broadcasted_iota(jnp.int32, (SEQ, SEQ), 0)
    col_id = lax.broadcasted_iota(jnp.int32, (SEQ, SEQ), 1)
    causal = row_id >= col_id
    dk = jnp.zeros((SEQ, HD), F32)
    dv = jnp.zeros((SEQ, HD), F32)
    dq_heads = []
    for h in range(2):
        g_head = gc_ref[:, h * HD : (h + 1) * HD]
        scores = jnp.where(causal, dot_rows(q_heads[h], k_head) * SCALE, -1e30)
        weights = jnp.exp(scores - jnp.max(scores, axis=1, keepdims=True))
        probs = weights / jnp.sum(weights, axis=1, keepdims=True)
        grad_probs = dot_rows(g_head, v_head)
        delta = jnp.sum(probs * grad_probs, axis=1, keepdims=True)
        grad_scores = (probs * (grad_probs - delta) * SCALE).astype(BF16)
        dq = dot(grad_scores, k_head)
        dq_heads.append(rotate(dq, cos_ref[...], -sin_ref[...]).astype(BF16))
        dk = dk + dot_columns(grad_scores, q_heads[h])
        dv = dv + dot_columns(probs.astype(BF16), g_head)

    def pack(r):
        def shifted(value, amount):
            amount = amount % 128
            return pltpu.roll(value, amount, 1) if amount else value

        total = shifted(dk[:128], -32 * r)
        total = jnp.where(lane // 32 == 1, shifted(dv[:128], 32 - 32 * r), total)
        total = jnp.where(lane // 32 == 2, shifted(dk[128:], 64 - 32 * r), total)
        return jnp.where(lane // 32 == 3, shifted(dv[128:], 96 - 32 * r), total)

    for r in range(4):
        dks[r] = pack(r)
    for step in (1, 2, 3):
        dkr[step - 1] = dks[peer(step)].astype(BF16)

    def dk_copy(step):
        return remote(dkr.at[step - 1], dkr.at[step + 2], dk_send.at[step - 1], dk_recv.at[step - 1], group[step])

    for step in (1, 2, 3):
        dk_copy(step).start()

    def ordered(value, core):
        return jnp.concatenate(
            [value[16 * (8 * b + 2 * a + core) : 16 * (8 * b + 2 * a + core) + 16] for a in range(NX) for b in range(2)],
            axis=0,
        )

    def place(value, lanes):
        for core in range(2):
            part = ordered(value, core)
            start = pl.multiple_of(jnp.where(c == core, 128, 0), 128)
            A[pl.ds(start, 128), lanes * 128 : lanes * 128 + 128] = part

    place(dq_heads[0], 0)
    place(dq_heads[1], 1)
    for step in (1, 2, 3):
        dk_copy(step).wait()
    dkv = dks[rank] + dkr[3].astype(F32) + dkr[4].astype(F32) + dkr[5].astype(F32)
    dkv = rotate(dkv, kcos_ref[rank], -ksin_ref[rank])
    turned = pltpu.roll(dkv, 64, 1)
    place(jnp.concatenate([jnp.where(lane < 64, dkv, 0.0), jnp.where(lane < 64, turned, 0.0)], axis=0).astype(BF16), 2)
    place(jnp.concatenate([jnp.where(lane < 64, 0.0, turned), jnp.where(lane < 64, 0.0, dkv)], axis=0).astype(BF16), 3)

    def sib_copy(m):
        return remote(sibs.at[m], sibr.at[m], sib_send.at[m], sib_recv.at[m], sibling)

    def relay_up(m):
        return remote(S.at[m, 0, xo], xrelay.at[m, 0], x_send.at[0, m], x_recv.at[0, m], to_xr)

    def relay_down(m):
        return remote(S.at[m, 1, xo], xrelay.at[m, 1], x_send.at[1, m], x_recv.at[1, m], to_xl)

    def direct_up(m):
        return remote(S.at[m, 1, xr], xin.at[m, 0], x_send.at[2, m], x_recv.at[2, m], to_xr)

    def direct_down(m):
        return remote(S.at[m, 0, xl], xin.at[m, 1], x_send.at[3, m], x_recv.at[3, m], to_xl)

    def summed_up(m):
        return remote(S.at[m, 0, xr], xin.at[m, 2], x_send.at[4, m], x_recv.at[4, m], to_xr)

    def summed_down(m):
        return remote(S.at[m, 1, xl], xin.at[m, 3], x_send.at[5, m], x_recv.at[5, m], to_xl)

    def far_copy(m):
        return remote(zsend.at[m], zin.at[m], z_send.at[m], z_recv.at[m], far)

    def term(m):
        dq = A[:, 0:256]
        dkv_a, dkv_b = A[:, 256:384], A[:, 384:512]
        for k in range(NY):
            i = m * NY + k
            weights = jnp.concatenate([W[i, 0:256, :], W[i, 256:512, :]], axis=1)
            both = W[i, 512:640, :]
            value = dot_rows(dq, weights)
            value = value + jnp.concatenate([dot_rows(dkv_a, both), dot_rows(dkv_b, both)], axis=1)
            columns = slice((k % 2) * 256, (k % 2) * 256 + 256)
            sibs[m, k // 2, :, columns] = value[:128].astype(BF16)
            own[m, k // 2, :, columns] = value[128:]
        sib_copy(m).start()

    def over_cores(m):
        sib_copy(m).wait_recv()
        for h in range(2):
            for a in range(NX):
                rows = slice(32 * a, 32 * a + 32)
                S[m, h, a] = (own[m, h, rows, :] + sibr[m, h, rows, :].astype(F32)).astype(BF16)
        relay_up(m).start()
        relay_down(m).start()
        direct_up(m).start()
        direct_down(m).start()

    def over_x(m):
        relay_up(m).wait_recv()
        S[m, 0, xr] = (S[m, 0, xr].astype(F32) + xrelay[m, 0].astype(F32)).astype(BF16)
        summed_up(m).start()
        relay_down(m).wait_recv()
        S[m, 1, xl] = (S[m, 1, xl].astype(F32) + xrelay[m, 1].astype(F32)).astype(BF16)
        summed_down(m).start()

    def at_owner_x(m):
        direct_up(m).wait_recv()
        direct_down(m).wait_recv()
        summed_up(m).wait_recv()
        summed_down(m).wait_recv()
        for h in range(2):
            first, second = (1, 2) if h == 0 else (0, 3)
            total = S[m, h, x].astype(F32) + xin[m, first].astype(F32) + xin[m, second].astype(F32)
            fs[m, 0, h] = total[0:16]
            fs[m, 1, h] = total[16:32]
        zsend[m] = fs[m, 1 - zh].astype(BF16)
        far_copy(m).start()

    own_rows = pl.ds(pl.multiple_of(tensor * 16, 16), 16)

    def columns_of(m, h):
        return pl.ds(pl.multiple_of(m * 1024 + h * 512, 512), 512)

    def at_owner(m, dots):
        far_copy(m).wait_recv()
        for h in range(2):
            columns = columns_of(m, h)
            scaled = (fs[m, zh, h] + zin[m, h].astype(F32)) * gain_ref[:, columns]
            G[m, h] = scaled
            dots = dots + scaled * hid[own_rows, columns].astype(F32)
        return dots

    def sum_step(n, dots):
        @pl.when(n < NZ)
        def _():
            term(n)

        @pl.when(jnp.logical_and(n >= 1, n < NZ + 1))
        def _():
            over_cores(n - 1)

        @pl.when(jnp.logical_and(n >= 2, n < NZ + 2))
        def _():
            over_x(n - 2)

        @pl.when(n >= 3)
        def _():
            at_owner_x(n - 3)

        return dots

    lax.fori_loop(0, NZ + 3, sum_step, 0)
    dots = lax.fori_loop(0, NZ, at_owner, jnp.zeros((16, 512), F32))
    mean_term = jnp.sum(dots, axis=1, keepdims=True) * (1.0 / D)
    own_hidden = hid[own_rows, :].astype(F32)
    inverse = lax.rsqrt(jnp.mean(own_hidden * own_hidden, axis=1, keepdims=True) + 1e-05)
    factor = inverse * inverse * mean_term
    for m in range(NZ):
        for h in range(2):
            columns = slice(m * 1024 + h * 512, m * 1024 + h * 512 + 512)
            value = inverse * (G[m, h] - own_hidden[:, columns] * factor)
            out_ref[:, columns] = value.astype(BF16)

    def gather_sent(j, carry):
        i = j * NY + y

        @pl.when(go_up(j))
        def _():
            block(i, up, 0).wait_send()

        @pl.when(go_down(j))
        def _():
            block(i, down, 4).wait_send()

        block(i, to_yr, 1).wait_send()
        block(i, to_yl, 2).wait_send()
        half_block(j * NY + yl, 0, to_yr).wait_send()
        half_block(j * NY + yr, 1, to_yl).wait_send()
        return carry

    lax.fori_loop(0, NZ, gather_sent, 0)

    def sum_sent(m, carry):
        for copy in (sib_copy, relay_up, relay_down, direct_up, direct_down, summed_up, summed_down, far_copy):
            copy(m).wait_send()
        return carry

    lax.fori_loop(0, NZ, sum_sent, 0)


def per_device(hidden, norm_gain, w_query, w_key, w_value, grad_context):
    tables = [jnp.asarray(table) for table in rotary_tables()]
    vmem = pl.BlockSpec(memory_space=pltpu.VMEM)
    hbm = pl.BlockSpec(memory_space=pl.ANY)
    dma = pltpu.SemaphoreType.DMA
    return pl.pallas_call(
        kernel,
        out_shape=jax.ShapeDtypeStruct((16, D), BF16),
        in_specs=[hbm, vmem, hbm, vmem, vmem, vmem, vmem, vmem, vmem, vmem],
        out_specs=vmem,
        scratch_shapes=[
            pltpu.VMEM((SEQ, D), BF16),
            pltpu.VMEM((SLOTS, ROWS, 128), BF16),
            pltpu.VMEM((SEQ, D), BF16),
            pltpu.VMEM((2, SEQ, HD), F32),
            pltpu.VMEM((2, SEQ, HD), F32),
            pltpu.VMEM((4, 128, 128), BF16),
            pltpu.VMEM((4, 128, 128), F32),
            pltpu.VMEM((6, 128, 128), BF16),
            pltpu.VMEM((SEQ, 512), BF16),
            pltpu.VMEM((NZ, 2, 128, 512), BF16),
            pltpu.VMEM((NZ, 2, 128, 512), BF16),
            pltpu.VMEM((NZ, 2, 128, 512), F32),
            pltpu.VMEM((NZ, 2, NX, 32, 512), BF16),
            pltpu.VMEM((NZ, 2, 32, 512), BF16),
            pltpu.VMEM((NZ, 4, 32, 512), BF16),
            pltpu.VMEM((NZ, 2, 2, 16, 512), F32),
            pltpu.VMEM((NZ, 2, 16, 512), BF16),
            pltpu.VMEM((NZ, 2, 16, 512), BF16),
            pltpu.VMEM((NZ, 2, 16, 512), F32),
            dma,
            dma((2,)),
            dma((SLOTS, 2)),
            dma((5, SLOTS)),
            dma((3,)),
            dma((3,)),
            dma((3,)),
            dma((3,)),
            dma((NZ,)),
            dma((NZ,)),
            dma((6, NZ)),
            dma((6, NZ)),
            dma((NZ,)),
            dma((NZ,)),
        ],
        compiler_params=pltpu.CompilerParams(
            collective_id=0, has_side_effects=True, vmem_limit_bytes=48 * 1024 * 1024
        ),
        name="attention_input_grad",
    )(hidden, norm_gain.reshape(1, D), w_query, w_key, w_value, grad_context, *tables)


def solution(mesh):
    in_specs = (
        P("dp", None),
        P(),
        P("dp", "tensor"),
        P("dp", "tensor"),
        P("dp", "tensor"),
        P("dp", "tensor"),
    )
    out_specs = P(("dp", "tensor"), None)
    return jax.shard_map(
        per_device, mesh=mesh, in_specs=in_specs, out_specs=out_specs, check_vma=False
    )
```

```python
import functools
import math

import jax
import jax.numpy as jnp
import numpy as np
from jax import lax
from jax.experimental import pallas as pl
from jax.experimental.pallas import tpu as pltpu
from jax.sharding import PartitionSpec as P

D = 8192
HD = 128
SEQ = 256
NZ, NY, NX = 8, 4, 4
SLOTS = NZ * NY
ROWS = 640
PARTS = 4
PART = ROWS // PARTS
LAG_B, LAG_C = 3, 8
ROPE_THETA = 500000.0
SCALE = 1.0 / math.sqrt(HD)
MESH = pl.DeviceIdType.MESH
F32, BF16 = jnp.float32, jnp.bfloat16


def rotary_tables():
    lane = np.arange(HD)
    frequency = np.exp((lane // 2) * (-2.0 * math.log(ROPE_THETA) / HD))
    angle = np.arange(SEQ)[:, None] * frequency[None, :]
    cosine = np.cos(angle)
    sine = np.sin(angle) * np.where(lane % 2 == 0, -1.0, 1.0)[None, :]
    packed_cos = np.ones((4, 128, 128))
    packed_sin = np.zeros((4, 128, 128))
    for rank in range(4):
        columns = slice(32 * rank, 32 * rank + 32)
        for part in range(2):
            rows = slice(128 * part, 128 * part + 128)
            packed_cos[rank, :, 64 * part : 64 * part + 32] = cosine[rows, columns]
            packed_sin[rank, :, 64 * part : 64 * part + 32] = sine[rows, columns]
    return [table.astype(np.float32) for table in (cosine, sine, packed_cos, packed_sin)]


def dot(left, right):
    return lax.dot_general(left, right, (((1,), (0,)), ((), ())), preferred_element_type=F32)


def dot_rows(left, right):
    return lax.dot_general(left, right, (((1,), (1,)), ((), ())), preferred_element_type=F32)


def dot_columns(left, right):
    return lax.dot_general(left, right, (((0,), (0,)), ((), ())), preferred_element_type=F32)


def lanes_of(value):
    return lax.broadcasted_iota(jnp.int32, value.shape, 1)


def rotate(value, cosine, sine):
    left = pltpu.roll(value, 127, 1)
    right = pltpu.roll(value, 1, 1)
    swapped = jnp.where(lanes_of(value) % 2 == 0, left, right)
    return value * cosine + swapped * sine


def kernel(
    hid_hbm, gain_hbm, wq_hbm, wk_hbm, wv_hbm, gc_hbm, cos_hbm, sin_hbm, kcos_hbm, ksin_hbm,
    out_ref,
    hid, gain, wkv, gc, cosine, sine, kcos, ksin, W, N, qacc, kvacc, kvs, dks, dkr, A,
    sibs, sibr, own, S, xrelay, xin, fs, zsend, zin, G,
    load_sem, ag_recv, ag_send, kv_recv, kv_send, dk_recv, dk_send,
    sib_recv, sib_send, x_recv, x_send, z_recv, z_send,
):
    dp = lax.axis_index("dp")
    tensor = lax.axis_index("tensor")
    z, y = dp // NY, dp % NY
    zh, x, c = tensor // 8, (tensor // 2) % NX, tensor % 2
    rank = tensor % 4
    yl, yr, yo = (y + 3) % 4, (y + 1) % 4, (y + 2) % 4
    xl, xr, xo = (x + 3) % 4, (x + 1) % 4, (x + 2) % 4

    def at_dp(zz, yy):
        return (zz * NY + yy, tensor)

    def at_tensor(zhh, xx, cc):
        return (dp, zhh * 8 + xx * 2 + cc)

    up, down = at_dp(z + 1, y), at_dp(z - 1, y)
    to_yl, to_yr = at_dp(z, yl), at_dp(z, yr)
    to_xl, to_xr = at_tensor(zh, xl, c), at_tensor(zh, xr, c)
    sibling = at_tensor(zh, x, 1 - c)
    far = at_tensor(1 - zh, x, c)
    x_pair = x + 1 - 2 * (x % 2)
    group = {1: sibling, 2: at_tensor(zh, x_pair, c), 3: at_tensor(zh, x_pair, 1 - c)}

    def remote(src, dst, send, recv, device):
        return pltpu.make_async_remote_copy(
            src_ref=src, dst_ref=dst, send_sem=send, recv_sem=recv, device_id=device, device_id_type=MESH
        )

    mine = z * NY + y

    def load(k, src, dst):
        return pltpu.make_async_copy(src, dst, load_sem.at[k])

    load_weights = [
        load(0, wq_hbm.at[:, pl.ds(0, 128)], W.at[mine, pl.ds(0, 256)]),
        load(1, wq_hbm.at[:, pl.ds(128, 128)], W.at[mine, pl.ds(256, 256)]),
        load(2, wk_hbm, wkv.at[0]),
        load(3, wv_hbm, wkv.at[1]),
    ]
    load_rows = [load(4, hid_hbm, hid), load(5, gain_hbm, gain)]
    load_rest = [
        load(6, gc_hbm, gc),
        load(7, cos_hbm, cosine),
        load(8, sin_hbm, sine),
        load(9, kcos_hbm.at[rank], kcos),
        load(10, ksin_hbm.at[rank], ksin),
    ]
    for copy in load_weights:
        copy.start()
    barrier = pltpu.get_barrier_semaphore()

    def greet(device):
        pl.semaphore_signal(barrier, inc=1, device_id=device, device_id_type=MESH)

    for device in (to_yl, to_yr, to_xl, to_xr, sibling, group[3], far):
        greet(device)

    @pl.when(z < NZ - 1)
    def _():
        greet(up)

    @pl.when(z > 0)
    def _():
        greet(down)

    for copy in load_rows + load_rest:
        copy.start()
    for copy in load_weights:
        copy.wait()
    wk, wv = wkv[0].astype(F32), wkv[1].astype(F32)
    packed = jnp.concatenate([wk[:, :128], wv[:, :128], wk[:, 128:], wv[:, 128:]], axis=0)
    W[mine, 512:640, :] = packed.T.astype(BF16)
    pl.semaphore_wait(barrier, 7 + jnp.where(z < NZ - 1, 1, 0) + jnp.where(z > 0, 1, 0))

    def block(i, p, device, kind):
        rows = pl.ds(p * PART, PART)
        return remote(W.at[i, rows], W.at[i, rows], ag_send.at[kind, i], ag_recv.at[i, p], device)

    def sent(i, rows, device, kind):
        return remote(W.at[i, rows], W.at[i, rows], ag_send.at[kind, i], ag_recv.at[i, 0], device)

    def plane(n):
        s = (n + 1) // 2
        return jnp.where(n % 2 == 1, z - s, z + s)

    def inside(j):
        return jnp.logical_and(j >= 0, j < NZ)

    def go_up(j):
        return jnp.logical_and(j <= z, z < NZ - 1)

    def go_down(j):
        return jnp.logical_and(j >= z, z > 0)

    def spread(j, p):
        i = j * NY + y

        @pl.when(go_up(j))
        def _():
            block(i, p, up, 0).start()

        @pl.when(go_down(j))
        def _():
            block(i, p, down, 4).start()

        block(i, p, to_yr, 1).start()
        block(i, p, to_yl, 2).start()

    def multiply(i):
        columns = pl.ds(pl.multiple_of(i * 256, 256), 256)
        rows = N[:, columns]
        qacc[0] += dot(rows, W[i, 0:256, :])
        qacc[1] += dot(rows, W[i, 256:512, :])
        both = W[i, 512:640, :]
        kvacc[0] += dot(rows[:, 0:128], both)
        kvacc[1] += dot(rows[:, 128:256], both)

    for p in range(PARTS):
        spread(z, p)
    qacc[...] = jnp.zeros_like(qacc)
    kvacc[...] = jnp.zeros_like(kvacc)
    for copy in load_rows:
        copy.wait()

    def norm_rows(b, carry):
        rows = pl.ds(pl.multiple_of(b * 16, 16), 16)
        values = hid[rows, :].astype(F32)
        inverse = lax.rsqrt(jnp.mean(values * values, axis=1, keepdims=True) + 1e-05)
        N[rows, :] = (values * inverse * gain[...]).astype(BF16)
        return carry

    lax.fori_loop(0, SEQ // 16, norm_rows, 0)

    def gather_step(n, carry):
        ja = plane(n)

        @pl.when(jnp.logical_and(inside(ja), jnp.logical_and(n > 0, n < 15)))
        def _():
            i = ja * NY + y
            for p in range(PARTS):
                block(i, p, up, 0).wait_recv()
                spread(ja, p)

        jb = plane(n - LAG_B)

        @pl.when(jnp.logical_and(inside(jb), jnp.logical_and(n >= LAG_B, n < 15 + LAG_B)))
        def _():
            i_left, i_right = jb * NY + yl, jb * NY + yr
            for p in range(PARTS):
                block(i_left, p, to_yr, 1).wait_recv()
                if p < PARTS // 2:
                    block(i_left, p, to_yr, 3).start()
                block(i_right, p, to_yl, 2).wait_recv()
                if p >= PARTS // 2:
                    block(i_right, p, to_yl, 3).start()
            multiply(jb * NY + y)
            multiply(i_left)
            multiply(i_right)

        jc = plane(n - LAG_C)

        @pl.when(jnp.logical_and(inside(jc), n >= LAG_C))
        def _():
            i = jc * NY + yo
            for p in range(PARTS):
                block(i, p, to_yr, 3).wait_recv()
            multiply(i)

        return carry

    lax.fori_loop(0, 15 + LAG_C, gather_step, 0)

    for copy in load_rest:
        copy.wait()

    def gather_sent(j, carry):
        i = j * NY + y
        whole = pl.ds(0, ROWS)

        @pl.when(go_up(j))
        def _():
            sent(i, whole, up, 0).wait_send()

        @pl.when(go_down(j))
        def _():
            sent(i, whole, down, 4).wait_send()

        sent(i, whole, to_yr, 1).wait_send()
        sent(i, whole, to_yl, 2).wait_send()
        sent(j * NY + yl, pl.ds(0, ROWS // 2), to_yr, 3).wait_send()
        sent(j * NY + yr, pl.ds(ROWS // 2, ROWS // 2), to_yl, 3).wait_send()
        return carry

    lane = lax.broadcasted_iota(jnp.int32, (128, 128), 1)
    kva, kvb = kvacc[0], kvacc[1]
    low = kva[:128] + pltpu.roll(kvb[:128], 64, 1)
    high = pltpu.roll(kva[128:], 64, 1) + kvb[128:]
    kv_own = rotate(jnp.where(lane < 64, low, high), kcos[...], ksin[...])
    kvs[rank] = kv_own.astype(BF16)

    def peer(step):
        if step == 1:
            return rank + 1 - 2 * (rank % 2)
        if step == 2:
            return (rank + 2) % 4
        return 3 - rank

    def kv_copy(step):
        return remote(kvs.at[rank], kvs.at[rank], kv_send.at[step - 1], kv_recv.at[step - 1], group[step])

    for step in (1, 2, 3):
        kv_copy(step).start()
    q_heads = []
    for h in range(2):
        q_heads.append(rotate(qacc[h], cosine[...], sine[...]).astype(BF16))
    for step in (1, 2, 3):
        kv_copy(step).wait()

    def unpack(shift):
        parts = []
        for part in range(2):
            total = jnp.zeros((128, 128), F32)
            for r in range(4):
                piece = kvs[r].astype(F32)
                amount = (32 * r - shift - 64 * part) % 128
                piece = pltpu.roll(piece, amount, 1) if amount else piece
                total = jnp.where(lane // 32 == r, piece, total)
            parts.append(total)
        return jnp.concatenate(parts, axis=0).astype(BF16)

    k_head, v_head = unpack(0), unpack(32)
    row_id = lax.broadcasted_iota(jnp.int32, (SEQ, SEQ), 0)
    col_id = lax.broadcasted_iota(jnp.int32, (SEQ, SEQ), 1)
    causal = row_id >= col_id
    dk = jnp.zeros((SEQ, HD), F32)
    dv = jnp.zeros((SEQ, HD), F32)
    dq_heads = []
    for h in range(2):
        g_head = gc[:, h * HD : (h + 1) * HD]
        scores = jnp.where(causal, dot_rows(q_heads[h], k_head) * SCALE, -1e30)
        weights = jnp.exp(scores - jnp.max(scores, axis=1, keepdims=True))
        probs = weights / jnp.sum(weights, axis=1, keepdims=True)
        grad_probs = dot_rows(g_head, v_head)
        delta = jnp.sum(probs * grad_probs, axis=1, keepdims=True)
        grad_scores = (probs * (grad_probs - delta) * SCALE).astype(BF16)
        dq = dot(grad_scores, k_head)
        dq_heads.append(rotate(dq, cosine[...], -sine[...]).astype(BF16))
        dk = dk + dot_columns(grad_scores, q_heads[h])
        dv = dv + dot_columns(probs.astype(BF16), g_head)

    def pack(r):
        def shifted(value, amount):
            amount = amount % 128
            return pltpu.roll(value, amount, 1) if amount else value

        total = shifted(dk[:128], -32 * r)
        total = jnp.where(lane // 32 == 1, shifted(dv[:128], 32 - 32 * r), total)
        total = jnp.where(lane // 32 == 2, shifted(dk[128:], 64 - 32 * r), total)
        return jnp.where(lane // 32 == 3, shifted(dv[128:], 96 - 32 * r), total)

    for r in range(4):
        dks[r] = pack(r)
    for step in (1, 2, 3):
        dkr[step - 1] = dks[peer(step)].astype(BF16)

    def dk_copy(step):
        return remote(dkr.at[step - 1], dkr.at[step + 2], dk_send.at[step - 1], dk_recv.at[step - 1], group[step])

    for step in (1, 2, 3):
        dk_copy(step).start()

    def ordered(value, core):
        return jnp.concatenate(
            [value[16 * (8 * b + 2 * a + core) : 16 * (8 * b + 2 * a + core) + 16] for a in range(NX) for b in range(2)],
            axis=0,
        )

    def place(value, lanes):
        for core in range(2):
            part = ordered(value, core)
            start = pl.multiple_of(jnp.where(c == core, 128, 0), 128)
            A[pl.ds(start, 128), lanes * 128 : lanes * 128 + 128] = part

    place(dq_heads[0], 0)
    place(dq_heads[1], 1)
    for step in (1, 2, 3):
        dk_copy(step).wait()
    dkv = dks[rank] + dkr[3].astype(F32) + dkr[4].astype(F32) + dkr[5].astype(F32)
    dkv = rotate(dkv, kcos[...], -ksin[...])
    turned = pltpu.roll(dkv, 64, 1)
    place(jnp.concatenate([jnp.where(lane < 64, dkv, 0.0), jnp.where(lane < 64, turned, 0.0)], axis=0).astype(BF16), 2)
    place(jnp.concatenate([jnp.where(lane < 64, 0.0, turned), jnp.where(lane < 64, 0.0, dkv)], axis=0).astype(BF16), 3)

    def sib_copy(m):
        return remote(sibs.at[m], sibr.at[m], sib_send.at[m], sib_recv.at[m], sibling)

    def relay_up(m):
        return remote(S.at[m, 0, xo], xrelay.at[m, 0], x_send.at[0, m], x_recv.at[0, m], to_xr)

    def relay_down(m):
        return remote(S.at[m, 1, xo], xrelay.at[m, 1], x_send.at[1, m], x_recv.at[1, m], to_xl)

    def direct_up(m):
        return remote(S.at[m, 1, xr], xin.at[m, 0], x_send.at[2, m], x_recv.at[2, m], to_xr)

    def direct_down(m):
        return remote(S.at[m, 0, xl], xin.at[m, 1], x_send.at[3, m], x_recv.at[3, m], to_xl)

    def summed_up(m):
        return remote(S.at[m, 0, xr], xin.at[m, 2], x_send.at[4, m], x_recv.at[4, m], to_xr)

    def summed_down(m):
        return remote(S.at[m, 1, xl], xin.at[m, 3], x_send.at[5, m], x_recv.at[5, m], to_xl)

    def far_copy(m):
        return remote(zsend.at[m], zin.at[m], z_send.at[m], z_recv.at[m], far)

    def term(m):
        dq = A[:, 0:256]
        dkv_a, dkv_b = A[:, 256:384], A[:, 384:512]
        for k in range(NY):
            i = m * NY + k
            weights = jnp.concatenate([W[i, 0:256, :], W[i, 256:512, :]], axis=1)
            both = W[i, 512:640, :]
            value = dot_rows(dq, weights)
            value = value + jnp.concatenate([dot_rows(dkv_a, both), dot_rows(dkv_b, both)], axis=1)
            columns = slice((k % 2) * 256, (k % 2) * 256 + 256)
            sibs[m, k // 2, :, columns] = value[:128].astype(BF16)
            own[m, k // 2, :, columns] = value[128:]
        sib_copy(m).start()

    def over_cores(m):
        sib_copy(m).wait_recv()
        for h in range(2):
            for a in range(NX):
                rows = slice(32 * a, 32 * a + 32)
                S[m, h, a] = (own[m, h, rows, :] + sibr[m, h, rows, :].astype(F32)).astype(BF16)
        relay_up(m).start()
        relay_down(m).start()
        direct_up(m).start()
        direct_down(m).start()

    def over_x(m):
        relay_up(m).wait_recv()
        S[m, 0, xr] = (S[m, 0, xr].astype(F32) + xrelay[m, 0].astype(F32)).astype(BF16)
        summed_up(m).start()
        relay_down(m).wait_recv()
        S[m, 1, xl] = (S[m, 1, xl].astype(F32) + xrelay[m, 1].astype(F32)).astype(BF16)
        summed_down(m).start()

    def at_owner_x(m):
        direct_up(m).wait_recv()
        direct_down(m).wait_recv()
        summed_up(m).wait_recv()
        summed_down(m).wait_recv()
        for h in range(2):
            first, second = (1, 2) if h == 0 else (0, 3)
            total = S[m, h, x].astype(F32) + xin[m, first].astype(F32) + xin[m, second].astype(F32)
            fs[m, 0, h] = total[0:16]
            fs[m, 1, h] = total[16:32]
        zsend[m] = fs[m, 1 - zh].astype(BF16)
        far_copy(m).start()

    own_rows = pl.ds(pl.multiple_of(tensor * 16, 16), 16)

    def columns_of(m, h):
        return pl.ds(pl.multiple_of(m * 1024 + h * 512, 512), 512)

    def at_owner(m, dots):
        far_copy(m).wait_recv()
        for h in range(2):
            columns = columns_of(m, h)
            scaled = (fs[m, zh, h] + zin[m, h].astype(F32)) * gain[:, columns]
            G[m, h] = scaled
            dots = dots + scaled * hid[own_rows, columns].astype(F32)
        return dots

    def sum_step(n, dots):
        @pl.when(n < NZ)
        def _():
            term(n)

        @pl.when(jnp.logical_and(n >= 1, n < NZ + 1))
        def _():
            over_cores(n - 1)

        @pl.when(jnp.logical_and(n >= 2, n < NZ + 2))
        def _():
            over_x(n - 2)

        @pl.when(n >= 3)
        def _():
            at_owner_x(n - 3)

        return dots

    lax.fori_loop(0, NZ + 3, sum_step, 0)
    dots = lax.fori_loop(0, NZ, at_owner, jnp.zeros((16, 512), F32))
    mean_term = jnp.sum(dots, axis=1, keepdims=True) * (1.0 / D)
    own_hidden = hid[own_rows, :].astype(F32)
    inverse = lax.rsqrt(jnp.mean(own_hidden * own_hidden, axis=1, keepdims=True) + 1e-05)
    factor = inverse * inverse * mean_term
    for m in range(NZ):
        for h in range(2):
            columns = slice(m * 1024 + h * 512, m * 1024 + h * 512 + 512)
            value = inverse * (G[m, h] - own_hidden[:, columns] * factor)
            out_ref[:, columns] = value.astype(BF16)

    lax.fori_loop(0, NZ, gather_sent, 0)

    def sum_sent(m, carry):
        for copy in (sib_copy, relay_up, relay_down, direct_up, direct_down, summed_up, summed_down, far_copy):
            copy(m).wait_send()
        return carry

    lax.fori_loop(0, NZ, sum_sent, 0)


def per_device(hidden, norm_gain, w_query, w_key, w_value, grad_context):
    tables = [jnp.asarray(table) for table in rotary_tables()]
    vmem = pl.BlockSpec(memory_space=pltpu.VMEM)
    hbm = pl.BlockSpec(memory_space=pl.ANY)
    dma = pltpu.SemaphoreType.DMA
    return pl.pallas_call(
        kernel,
        out_shape=jax.ShapeDtypeStruct((16, D), BF16),
        in_specs=[hbm] * 10,
        out_specs=vmem,
        scratch_shapes=[
            pltpu.VMEM((SEQ, D), BF16),
            pltpu.VMEM((1, D), F32),
            pltpu.VMEM((2, 32, 256), BF16),
            pltpu.VMEM((SEQ, 256), BF16),
            pltpu.VMEM((SEQ, HD), F32),
            pltpu.VMEM((SEQ, HD), F32),
            pltpu.VMEM((128, 128), F32),
            pltpu.VMEM((128, 128), F32),
            pltpu.VMEM((SLOTS, ROWS, 128), BF16),
            pltpu.VMEM((SEQ, D), BF16),
            pltpu.VMEM((2, SEQ, HD), F32),
            pltpu.VMEM((2, SEQ, HD), F32),
            pltpu.VMEM((4, 128, 128), BF16),
            pltpu.VMEM((4, 128, 128), F32),
            pltpu.VMEM((6, 128, 128), BF16),
            pltpu.VMEM((SEQ, 512), BF16),
            pltpu.VMEM((NZ, 2, 128, 512), BF16),
            pltpu.VMEM((NZ, 2, 128, 512), BF16),
            pltpu.VMEM((NZ, 2, 128, 512), F32),
            pltpu.VMEM((NZ, 2, NX, 32, 512), BF16),
            pltpu.VMEM((NZ, 2, 32, 512), BF16),
            pltpu.VMEM((NZ, 4, 32, 512), BF16),
            pltpu.VMEM((NZ, 2, 2, 16, 512), F32),
            pltpu.VMEM((NZ, 2, 16, 512), BF16),
            pltpu.VMEM((NZ, 2, 16, 512), BF16),
            pltpu.VMEM((NZ, 2, 16, 512), F32),
            dma((11,)),
            dma((SLOTS, PARTS)),
            dma((5, SLOTS)),
            dma((3,)),
            dma((3,)),
            dma((3,)),
            dma((3,)),
            dma((NZ,)),
            dma((NZ,)),
            dma((6, NZ)),
            dma((6, NZ)),
            dma((NZ,)),
            dma((NZ,)),
        ],
        compiler_params=pltpu.CompilerParams(
            collective_id=0, has_side_effects=True, vmem_limit_bytes=60 * 1024 * 1024
        ),
        name="attention_input_grad",
    )(hidden, norm_gain.reshape(1, D), w_query, w_key.T, w_value.T, grad_context, *tables)


def solution(mesh):
    in_specs = (
        P("dp", None),
        P(),
        P("dp", "tensor"),
        P("dp", "tensor"),
        P("dp", "tensor"),
        P("dp", "tensor"),
    )
    out_specs = P(("dp", "tensor"), None)
    return jax.shard_map(
        per_device, mesh=mesh, in_specs=in_specs, out_specs=out_specs, check_vma=False
    )
```

```python
import functools
import math

import jax
import jax.numpy as jnp
import numpy as np
from jax import lax
from jax.experimental import pallas as pl
from jax.experimental.pallas import tpu as pltpu
from jax.sharding import PartitionSpec as P

D = 8192
HD = 128
SEQ = 256
NZ, NY, NX = 8, 4, 4
PLANES = NZ // 2
SLOTS = PLANES * NY
ROWS = 640
PARTS = 4
PART = ROWS // PARTS
LAG_B, LAG_C = 2, 4
PAIR_STEP, SPREAD_STEP, PARTNER_STEP, PARTNER_PLANES = 4, 8, 9, 4
CHUNKS = 8
LAG_X, LAG_O = 2, 3
ROPE_THETA = 500000.0
SCALE = 1.0 / math.sqrt(HD)
MESH = pl.DeviceIdType.MESH
F32, BF16 = jnp.float32, jnp.bfloat16


def rotary_tables():
    lane = np.arange(HD)
    frequency = np.exp((lane // 2) * (-2.0 * math.log(ROPE_THETA) / HD))
    angle = np.arange(SEQ)[:, None] * frequency[None, :]
    cosine = np.cos(angle)
    sine = np.sin(angle) * np.where(lane % 2 == 0, -1.0, 1.0)[None, :]
    packed_cos = np.ones((4, 128, 128))
    packed_sin = np.zeros((4, 128, 128))
    for rank in range(4):
        columns = slice(32 * rank, 32 * rank + 32)
        for part in range(2):
            rows = slice(128 * part, 128 * part + 128)
            packed_cos[rank, :, 64 * part : 64 * part + 32] = cosine[rows, columns]
            packed_sin[rank, :, 64 * part : 64 * part + 32] = sine[rows, columns]
    return [table.astype(np.float32) for table in (cosine, sine, packed_cos, packed_sin)]


def dot(left, right):
    return lax.dot_general(left, right, (((1,), (0,)), ((), ())), preferred_element_type=F32)


def dot_rows(left, right):
    return lax.dot_general(left, right, (((1,), (1,)), ((), ())), preferred_element_type=F32)


def dot_columns(left, right):
    return lax.dot_general(left, right, (((0,), (0,)), ((), ())), preferred_element_type=F32)


def lanes_of(value):
    return lax.broadcasted_iota(jnp.int32, value.shape, 1)


def rotate(value, cosine, sine):
    left = pltpu.roll(value, 127, 1)
    right = pltpu.roll(value, 1, 1)
    swapped = jnp.where(lanes_of(value) % 2 == 0, left, right)
    return value * cosine + swapped * sine


def kernel(
    hid_hbm, gain_hbm, wq_hbm, wk_hbm, wv_hbm, gc_hbm, cos_hbm, sin_hbm, kcos_hbm, ksin_hbm,
    out_ref,
    hid, gain, wkv, gc, cosine, sine, kcos, ksin, W, N, given, qacc, kvacc, qs, qr, ks, kr,
    kvs, dks, dkr, AQ, AK, dkvs, T, sibs, sibr, own, S, xin, fs, zsend, zin, ps, pr, G, dots,
    load_sem, ag_recv, ag_send, ag_sent, n_recv, n_sent, q_recv, q_send, kv_recv, kv_send, dk_recv, dk_send,
    a_recv, a_send, sib_recv, sib_send, x_recv, x_send, z_recv, z_send, p_recv, p_send,
):
    dp = lax.axis_index("dp")
    tensor = lax.axis_index("tensor")
    z, y = dp // NY, dp % NY
    side, zz = z % 2, z // 2
    zh, x, c = tensor // 8, (tensor // 2) % NX, tensor % 2
    rank = tensor % 4
    share = tensor % 8
    yl, yr, yo = (y + 3) % 4, (y + 1) % 4, (y + 2) % 4
    xl, xr, xo = (x + 3) % 4, (x + 1) % 4, (x + 2) % 4

    def at_dp(zz, yy):
        return (zz * NY + yy, tensor)

    def at_tensor(zhh, xx, cc):
        return (dp, zhh * 8 + xx * 2 + cc)

    up, down = at_dp(z + 2, y), at_dp(z - 2, y)
    pair = at_dp(z + 1 - 2 * side, y)
    to_yl, to_yr = at_dp(z, yl), at_dp(z, yr)
    to_xl, to_xr, to_xo = at_tensor(zh, xl, c), at_tensor(zh, xr, c), at_tensor(zh, xo, c)
    sibling = at_tensor(zh, x, 1 - c)
    far = at_tensor(1 - zh, x, c)
    x_pair = x + 1 - 2 * (x % 2)
    group = {1: sibling, 2: at_tensor(zh, x_pair, c), 3: at_tensor(zh, x_pair, 1 - c)}

    def remote(src, dst, send, recv, device):
        return pltpu.make_async_remote_copy(
            src_ref=src, dst_ref=dst, send_sem=send, recv_sem=recv, device_id=device, device_id_type=MESH
        )

    def plane_start(j, which):
        return (2 * j + which) * 1024

    mine = zz * NY + y

    def load(k, src, dst):
        return pltpu.make_async_copy(src, dst, load_sem.at[k])

    load_weights = [
        load(0, wq_hbm.at[:, pl.ds(0, 128)], W.at[mine, pl.ds(0, 256)]),
        load(1, wq_hbm.at[:, pl.ds(128, 128)], W.at[mine, pl.ds(256, 256)]),
        load(2, wk_hbm, wkv.at[0]),
        load(3, wv_hbm, wkv.at[1]),
    ]
    load_rows = [load(4, hid_hbm, hid), load(5, gain_hbm, gain)]
    load_rest = [
        load(6, gc_hbm, gc),
        load(7, cos_hbm, cosine),
        load(8, sin_hbm, sine),
        load(9, kcos_hbm.at[rank], kcos),
        load(10, ksin_hbm.at[rank], ksin),
    ]
    for copy in load_weights:
        copy.start()
    barrier = pltpu.get_barrier_semaphore()

    def greet(device):
        pl.semaphore_signal(barrier, inc=1, device_id=device, device_id_type=MESH)

    for device in (to_yl, to_yr, to_xl, to_xr, to_xo, sibling, group[3], far, pair):
        greet(device)

    @pl.when(zz < PLANES - 1)
    def _():
        greet(up)

    @pl.when(zz > 0)
    def _():
        greet(down)

    for copy in load_rows + load_rest:
        copy.start()
    for copy in load_weights:
        copy.wait()
    wk, wv = wkv[0].astype(F32), wkv[1].astype(F32)
    packed = jnp.concatenate([wk[:, :128], wv[:, :128], wk[:, 128:], wv[:, 128:]], axis=0)
    W[mine, 512:640, :] = packed.T.astype(BF16)
    pl.semaphore_wait(barrier, 9 + jnp.where(zz < PLANES - 1, 1, 0) + jnp.where(zz > 0, 1, 0))

    def block(i, p, device, kind):
        rows = pl.ds(p * PART, PART)
        if kind in (0, 4):
            send = ag_send.at[kind // 4, i]
        elif kind == 3:
            send = ag_sent.at[2 + p // (PARTS // 2)]
        else:
            send = ag_sent.at[kind - 1]
        return remote(W.at[i, rows], W.at[i, rows], send, ag_recv.at[i, p], device)

    def sent(src, send, device):
        return remote(src, src, send, ag_recv.at[0, 0], device)

    def plane(n):
        s = (n + 1) // 2
        return jnp.where(n % 2 == 1, zz - s, zz + s)

    def inside(j):
        return jnp.logical_and(j >= 0, j < PLANES)

    def go_up(j):
        return jnp.logical_and(j <= zz, zz < PLANES - 1)

    def go_down(j):
        return jnp.logical_and(j >= zz, zz > 0)

    def spread(j, p):
        i = j * NY + y

        @pl.when(go_up(j))
        def _():
            block(i, p, up, 0).start()

        @pl.when(go_down(j))
        def _():
            block(i, p, down, 4).start()

        block(i, p, to_yr, 1).start()
        block(i, p, to_yl, 2).start()

    def rows_of(which, i):
        return N[which, i // 2, :, pl.ds(pl.multiple_of((i % 2) * 256, 256), 256)]

    def multiply_q(which, i):
        rows = rows_of(which, i)
        qacc[which, 0] += dot(rows, W[i, 0:256, :])
        qacc[which, 1] += dot(rows, W[i, 256:512, :])

    def multiply_kv(which, i):
        rows = rows_of(which, i)
        both = W[i, 512:640, :]
        kvacc[which, 0] += dot(rows[:, 0:128], both)
        kvacc[which, 1] += dot(rows[:, 128:256], both)

    def multiply(i):
        multiply_q(0, i)
        multiply_kv(0, i)

    for p in range(PARTS):
        spread(zz, p)
    qacc[...] = jnp.zeros_like(qacc)
    kvacc[...] = jnp.zeros_like(kvacc)

    given_start = pl.multiple_of(plane_start(share // 2, 1 - side) + (share % 2) * 512, 512)

    def norm_rows(b):
        rows = pl.ds(pl.multiple_of(b * 16, 16), 16)
        values = hid[rows, :].astype(F32)
        inverse = lax.rsqrt(jnp.mean(values * values, axis=1, keepdims=True) + 1e-05)

        def normed(start):
            columns = pl.ds(start, 512)
            return (hid[rows, columns].astype(F32) * inverse * gain[:, columns]).astype(BF16)

        given[rows, :] = normed(given_start)
        for e in range(8):
            start = pl.multiple_of(plane_start(e // 2, side) + (e % 2) * 512, 512)
            N[0, e, rows, :] = normed(start)

    def quarter(r):
        return pl.ds(pl.multiple_of(r * 64, 64), 64)

    def give(r):
        return remote(given.at[quarter(r)], N.at[1, share, quarter(r)], n_sent.at[0], n_recv.at[share, r], pair)

    def hand(kind, e, r, device):
        ref = N.at[1, e, quarter(r)]
        return remote(ref, ref, n_sent.at[kind], n_recv.at[e, r], device)

    for copy in load_rows:
        copy.wait()

    def norm_step(r, carry):
        def inner(b, inside_carry):
            norm_rows(r * 4 + b)
            return inside_carry

        lax.fori_loop(0, 4, inner, 0)
        give(r).start()
        return carry

    lax.fori_loop(0, 4, norm_step, 0)

    def spread_given(r, carry):
        give(r).wait_recv()
        hand(1, share, r, to_xr).start()
        hand(2, share, r, to_xl).start()
        hand(3, share, r, to_xo).start()
        hand(4, share, r, sibling).start()
        return carry

    def pass_given(r, carry):
        for xx, device in ((xl, to_xr), (xr, to_xl), (xo, to_xo)):
            e = xx * 2 + c
            hand(1, e, r, device).wait_recv()
            hand(4, e, r, sibling).start()
        return carry

    def wait_given(r, carry):
        for xx in range(NX):
            hand(4, xx * 2 + 1 - c, r, sibling).wait_recv()
        return carry

    def partner_planes(product, first, last):
        def step(n, carry):
            j = plane(n)

            @pl.when(inside(j))
            def _():
                for k in range(NY):
                    product(1, j * NY + k)

            return carry

        lax.fori_loop(first, last, step, 0)

    def gather_step(n, carry):
        @pl.when(n == PAIR_STEP)
        def _():
            lax.fori_loop(0, 4, spread_given, 0)

        @pl.when(n == SPREAD_STEP)
        def _():
            lax.fori_loop(0, 4, pass_given, 0)

        ja = plane(n)

        @pl.when(jnp.logical_and(inside(ja), n < 2 * PLANES - 1))
        def _():
            i = ja * NY + y
            for p in range(PARTS):
                block(i, p, up, 0).wait_recv()
                spread(ja, p)

        jb = plane(n - LAG_B)

        @pl.when(jnp.logical_and(inside(jb), jnp.logical_and(n >= LAG_B, n < 2 * PLANES - 1 + LAG_B)))
        def _():
            i_left, i_right = jb * NY + yl, jb * NY + yr
            for p in range(PARTS):
                block(i_left, p, to_yr, 1).wait_recv()
                if p < PARTS // 2:
                    block(i_left, p, to_yr, 3).start()
                block(i_right, p, to_yl, 2).wait_recv()
                if p >= PARTS // 2:
                    block(i_right, p, to_yl, 3).start()
            multiply(jb * NY + y)
            multiply(i_left)
            multiply(i_right)

        jc = plane(n - LAG_C)

        @pl.when(jnp.logical_and(inside(jc), n >= LAG_C))
        def _():
            i = jc * NY + yo
            for p in range(PARTS):
                block(i, p, to_yr, 3).wait_recv()
            multiply(i)

        @pl.when(n == PARTNER_STEP)
        def _():
            lax.fori_loop(0, 4, wait_given, 0)
            partner_planes(multiply_q, 0, PARTNER_PLANES)
            partner_planes(multiply_kv, 0, PARTNER_PLANES)

        return carry

    lax.fori_loop(1, 2 * PLANES - 1 + LAG_C, gather_step, 0)

    for copy in load_rest:
        copy.wait()

    def gather_sent():
        def chain_sent(j, carry):
            i = j * NY + y

            @pl.when(go_up(j))
            def _():
                sent(W.at[i], ag_send.at[0, i], up).wait_send()

            @pl.when(go_down(j))
            def _():
                sent(W.at[i], ag_send.at[1, i], down).wait_send()

            return carry

        lax.fori_loop(0, PLANES, chain_sent, 0)
        all_blocks, all_halves = W.at[pl.ds(0, PLANES)], W.at[pl.ds(0, PLANES), pl.ds(0, ROWS // 2)]
        sent(all_blocks, ag_sent.at[0], to_yr).wait_send()
        sent(all_blocks, ag_sent.at[1], to_yl).wait_send()
        sent(all_halves, ag_sent.at[2], to_yr).wait_send()
        sent(all_halves, ag_sent.at[3], to_yl).wait_send()
        sent(given, n_sent.at[0], pair).wait_send()
        for kind, device in ((1, to_xr), (2, to_xl), (3, to_xo)):
            sent(given, n_sent.at[kind], device).wait_send()
        sent(N.at[1, pl.ds(0, 4)], n_sent.at[4], sibling).wait_send()

    lane = lax.broadcasted_iota(jnp.int32, (128, 128), 1)

    def pack_kv(which):
        kva, kvb = kvacc[which, 0], kvacc[which, 1]
        low = kva[:128] + pltpu.roll(kvb[:128], 64, 1)
        high = pltpu.roll(kva[128:], 64, 1) + kvb[128:]
        return jnp.where(lane < 64, low, high)

    def ks_copy():
        return remote(ks, kr, q_send.at[0], q_recv.at[0], pair)

    def qs_copy(h):
        return remote(qs.at[h], qr.at[h], q_send.at[1 + h], q_recv.at[1 + h], pair)

    partner_planes(multiply_kv, PARTNER_PLANES, 2 * PLANES - 1)
    ks[...] = pack_kv(1).astype(BF16)
    ks_copy().start()
    partner_planes(multiply_q, PARTNER_PLANES, 2 * PLANES - 1)
    for h in range(2):
        qs[h] = qacc[1, h].astype(BF16)
        qs_copy(h).start()

    kv_mine = pack_kv(0)
    gather_sent()
    ks_copy().wait()
    kv_own = rotate(kv_mine + kr[...].astype(F32), kcos[...], ksin[...])
    kvs[rank] = kv_own.astype(BF16)

    def peer(step):
        if step == 1:
            return rank + 1 - 2 * (rank % 2)
        if step == 2:
            return (rank + 2) % 4
        return 3 - rank

    def kv_copy(step):
        return remote(kvs.at[rank], kvs.at[rank], kv_send.at[step - 1], kv_recv.at[step - 1], group[step])

    for step in (1, 2, 3):
        kv_copy(step).start()
    q_heads = []
    for h in range(2):
        qs_copy(h).wait()
        q_sum = qacc[0, h] + qr[h].astype(F32)
        q_heads.append(rotate(q_sum, cosine[...], sine[...]).astype(BF16))
    for step in (1, 2, 3):
        kv_copy(step).wait()

    def unpack(shift):
        parts = []
        for part in range(2):
            total = jnp.zeros((128, 128), F32)
            for r in range(4):
                piece = kvs[r].astype(F32)
                amount = (32 * r - shift - 64 * part) % 128
                piece = pltpu.roll(piece, amount, 1) if amount else piece
                total = jnp.where(lane // 32 == r, piece, total)
            parts.append(total)
        return jnp.concatenate(parts, axis=0).astype(BF16)

    k_head, v_head = unpack(0), unpack(32)
    row_id = lax.broadcasted_iota(jnp.int32, (SEQ, SEQ), 0)
    col_id = lax.broadcasted_iota(jnp.int32, (SEQ, SEQ), 1)
    causal = row_id >= col_id
    dk = jnp.zeros((SEQ, HD), F32)
    dv = jnp.zeros((SEQ, HD), F32)
    dq_heads = []
    for h in range(2):
        g_head = gc[:, h * HD : (h + 1) * HD]
        scores = jnp.where(causal, dot_rows(q_heads[h], k_head) * SCALE, -1e30)
        weights = jnp.exp(scores - jnp.max(scores, axis=1, keepdims=True))
        probs = weights / jnp.sum(weights, axis=1, keepdims=True)
        grad_probs = dot_rows(g_head, v_head)
        delta = jnp.sum(probs * grad_probs, axis=1, keepdims=True)
        grad_scores = (probs * (grad_probs - delta) * SCALE).astype(BF16)
        dq = dot(grad_scores, k_head)
        dq_heads.append(rotate(dq, cosine[...], -sine[...]).astype(BF16))
        dk = dk + dot_columns(grad_scores, q_heads[h])
        dv = dv + dot_columns(probs.astype(BF16), g_head)

    def pack(r):
        def shifted(value, amount):
            amount = amount % 128
            return pltpu.roll(value, amount, 1) if amount else value

        total = shifted(dk[:128], -32 * r)
        total = jnp.where(lane // 32 == 1, shifted(dv[:128], 32 - 32 * r), total)
        total = jnp.where(lane // 32 == 2, shifted(dk[128:], 64 - 32 * r), total)
        return jnp.where(lane // 32 == 3, shifted(dv[128:], 96 - 32 * r), total)

    for r in range(4):
        dks[r] = pack(r)
    for step in (1, 2, 3):
        dkr[step - 1] = dks[peer(step)].astype(BF16)

    def dk_copy(step):
        return remote(dkr.at[step - 1], dkr.at[step + 2], dk_send.at[step - 1], dk_recv.at[step - 1], group[step])

    for step in (1, 2, 3):
        dk_copy(step).start()

    def ordered(value, core):
        return jnp.concatenate(
            [value[16 * (8 * b + 2 * a + core) : 16 * (8 * b + 2 * a + core) + 16] for a in range(NX) for b in range(2)],
            axis=0,
        )

    def place(ref, value):
        for core in range(2):
            start = pl.multiple_of(jnp.where(c == core, 128, 0), 128)
            ref[pl.ds(start, 128), :] = ordered(value, core)

    def place_kv(which, value):
        turned = pltpu.roll(value, 64, 1)
        first = jnp.concatenate([jnp.where(lane < 64, value, 0.0), jnp.where(lane < 64, turned, 0.0)], axis=0)
        second = jnp.concatenate([jnp.where(lane < 64, 0.0, turned), jnp.where(lane < 64, 0.0, value)], axis=0)
        place(AK.at[which, 0], first.astype(BF16))
        place(AK.at[which, 1], second.astype(BF16))

    def aq_copy():
        return remote(AQ.at[0], AQ.at[1], a_send.at[0], a_recv.at[0], pair)

    def ak_copy():
        return remote(dkvs.at[0], dkvs.at[1], a_send.at[1], a_recv.at[1], pair)

    place(AQ.at[0], jnp.concatenate(dq_heads, axis=1))
    aq_copy().start()

    def weights_q(i):
        return jnp.concatenate([W[i, 0:256, :], W[i, 256:512, :]], axis=1)

    def query_term(j, carry):
        dq = AQ[0]
        for k in range(NY):
            T[j, k] = dot_rows(dq, weights_q(j * NY + k))
        return carry

    lax.fori_loop(0, PLANES, query_term, 0)
    for step in (1, 2, 3):
        dk_copy(step).wait()
    dkv = dks[rank] + dkr[3].astype(F32) + dkr[4].astype(F32) + dkr[5].astype(F32)
    dkv = rotate(dkv, kcos[...], -ksin[...]).astype(BF16)
    dkvs[0] = dkv
    ak_copy().start()
    place_kv(0, dkv.astype(F32))

    def sib_copy(m):
        return remote(sibs.at[m], sibr.at[m], sib_send.at[0], sib_recv.at[m], sibling)

    def x_copy(kind, m):
        x_dst, h, device = ((xo, 0, to_xr), (xo, 1, to_xl), (xr, 1, to_xr), (xl, 0, to_xl), (xr, 0, to_xr), (xl, 1, to_xl))[kind]
        return remote(S.at[m, x_dst, h], xin.at[m, kind], x_send.at[kind], x_recv.at[m, kind], device)

    def far_copy(m):
        return remote(zsend.at[m], zin.at[m], z_send.at[0], z_recv.at[m], far)

    def chunk(m):
        partner = jnp.logical_and(m >= 2, m < 6)
        return partner, jnp.where(m < 2, m, jnp.where(m < 6, m - 2, m - 4))

    def term(m):
        partner, j = chunk(m)

        def add_term(which):
            dkv_a, dkv_b = AK[which, 0], AK[which, 1]
            for k in range(NY):
                i = j * NY + k
                both = W[i, 512:640, :]
                base = T[j, k] if which == 0 else dot_rows(AQ[1], weights_q(i))
                value = base + jnp.concatenate([dot_rows(dkv_a, both), dot_rows(dkv_b, both)], axis=1)
                columns = slice((k % 2) * 256, (k % 2) * 256 + 256)
                sibs[m, k // 2, :, columns] = value[:128].astype(BF16)
                own[m, k // 2, :, columns] = value[128:]

        @pl.when(jnp.logical_not(partner))
        def _():
            add_term(0)

        @pl.when(partner)
        def _():
            add_term(1)

        sib_copy(m).start()

    def over_cores(m):
        sib_copy(m).wait_recv()
        for h in range(2):
            for a in range(NX):
                rows = slice(32 * a, 32 * a + 32)
                S[m, a, h] = (own[m, h, rows, :] + sibr[m, h, rows, :].astype(F32)).astype(BF16)

        for kind in (0, 1, 2, 3):
            x_copy(kind, m).start()

    def over_x(m):
        x_copy(0, m).wait_recv()
        S[m, xr, 0] = (S[m, xr, 0].astype(F32) + xin[m, 0].astype(F32)).astype(BF16)
        x_copy(4, m).start()
        x_copy(1, m).wait_recv()
        S[m, xl, 1] = (S[m, xl, 1].astype(F32) + xin[m, 1].astype(F32)).astype(BF16)
        x_copy(5, m).start()

    def send_far(m, totals):
        for h in range(2):
            fs[m, 0, h] = totals[h][0:16]
            fs[m, 1, h] = totals[h][16:32]
        zsend[m] = fs[m, 1 - zh].astype(BF16)
        far_copy(m).start()

    def at_owner_x(m):
        for kind in (2, 3, 4, 5):
            x_copy(kind, m).wait_recv()
        totals = [
            S[m, x, 0].astype(F32) + xin[m, 3].astype(F32) + xin[m, 4].astype(F32),
            S[m, x, 1].astype(F32) + xin[m, 2].astype(F32) + xin[m, 5].astype(F32),
        ]
        send_far(m, totals)

    own_rows = pl.ds(pl.multiple_of(tensor * 16, 16), 16)

    def pair_copy(j):
        return remote(ps.at[j], pr.at[j], p_send.at[0], p_recv.at[j], pair)

    def scale_plane(j, which, h, value, dots):
        columns = pl.ds(pl.multiple_of(plane_start(j, which) + h * 512, 512), 512)
        scaled = value * gain[:, columns]
        G[2 * j + which, h] = scaled
        dots[...] += scaled * hid[own_rows, columns].astype(F32)

    def at_owner(m, carry):
        partner, j = chunk(m)
        far_copy(m).wait_recv()

        @pl.when(jnp.logical_not(partner))
        def _():
            for h in range(2):
                scale_plane(j, side, h, fs[m, zh, h] + zin[m, h].astype(F32), dots)

        @pl.when(partner)
        def _():
            ps[j] = (fs[m, zh] + zin[m].astype(F32)).astype(BF16)
            pair_copy(j).start()

        return carry

    def from_partner(j, carry):
        pair_copy(j).wait_recv()
        for h in range(2):
            scale_plane(j, 1 - side, h, pr[j, h].astype(F32), dots)
        return carry

    dots[...] = jnp.zeros_like(dots)

    def sum_step(n, carry):
        @pl.when(n == 2)
        def _():
            aq_copy().wait()
            ak_copy().wait()
            place_kv(1, dkvs[1].astype(F32))

        @pl.when(n < CHUNKS)
        def _():
            term(n)

        @pl.when(jnp.logical_and(n >= 1, n < CHUNKS + 1))
        def _():
            over_cores(n - 1)

        @pl.when(jnp.logical_and(n >= LAG_X, n < CHUNKS + LAG_X))
        def _():
            over_x(n - LAG_X)

        @pl.when(n >= LAG_O)
        def _():
            at_owner_x(n - LAG_O)

        return carry

    lax.fori_loop(0, CHUNKS + LAG_O, sum_step, 0)

    remote(sibs, sibr, sib_send.at[0], sib_recv.at[0], sibling).wait_send()
    for kind in range(6):
        x_dst = (to_xr, to_xl)[kind % 2]
        remote(S.at[:, 0, 0], xin.at[:, 0], x_send.at[kind], x_recv.at[0, 0], x_dst).wait_send()
    lax.fori_loop(0, 6, at_owner, 0)
    lax.fori_loop(0, PLANES, from_partner, 0)
    lax.fori_loop(6, CHUNKS, at_owner, 0)
    mean_term = jnp.sum(dots[...], axis=1, keepdims=True) * (1.0 / D)
    own_hidden = hid[own_rows, :].astype(F32)
    inverse = lax.rsqrt(jnp.mean(own_hidden * own_hidden, axis=1, keepdims=True) + 1e-05)
    factor = inverse * inverse * mean_term
    for m in range(NZ):
        for h in range(2):
            columns = slice(m * 1024 + h * 512, m * 1024 + h * 512 + 512)
            value = inverse * (G[m, h] - own_hidden[:, columns] * factor)
            out_ref[:, columns] = value.astype(BF16)

    remote(zsend, zin, z_send.at[0], z_recv.at[0], far).wait_send()
    remote(ps, pr, p_send.at[0], p_recv.at[0], pair).wait_send()


def per_device(hidden, norm_gain, w_query, w_key, w_value, grad_context):
    tables = [jnp.asarray(table) for table in rotary_tables()]
    vmem = pl.BlockSpec(memory_space=pltpu.VMEM)
    hbm = pl.BlockSpec(memory_space=pl.ANY)
    dma = pltpu.SemaphoreType.DMA
    return pl.pallas_call(
        kernel,
        out_shape=jax.ShapeDtypeStruct((16, D), BF16),
        in_specs=[hbm] * 10,
        out_specs=vmem,
        scratch_shapes=[
            pltpu.VMEM((SEQ, D), BF16),
            pltpu.VMEM((1, D), F32),
            pltpu.VMEM((2, 32, 256), BF16),
            pltpu.VMEM((SEQ, 256), BF16),
            pltpu.VMEM((SEQ, HD), F32),
            pltpu.VMEM((SEQ, HD), F32),
            pltpu.VMEM((128, 128), F32),
            pltpu.VMEM((128, 128), F32),
            pltpu.VMEM((SLOTS, ROWS, 128), BF16),
            pltpu.VMEM((2, 8, SEQ, 512), BF16),
            pltpu.VMEM((SEQ, 512), BF16),
            pltpu.VMEM((2, 2, SEQ, HD), F32),
            pltpu.VMEM((2, 2, SEQ, HD), F32),
            pltpu.VMEM((2, SEQ, HD), BF16),
            pltpu.VMEM((2, SEQ, HD), BF16),
            pltpu.VMEM((128, 128), BF16),
            pltpu.VMEM((128, 128), BF16),
            pltpu.VMEM((4, 128, 128), BF16),
            pltpu.VMEM((4, 128, 128), F32),
            pltpu.VMEM((6, 128, 128), BF16),
            pltpu.VMEM((2, SEQ, 256), BF16),
            pltpu.VMEM((2, 2, SEQ, 128), BF16),
            pltpu.VMEM((2, 128, 128), BF16),
            pltpu.VMEM((PLANES, NY, SEQ, 256), F32),
            pltpu.VMEM((CHUNKS, 2, 128, 512), BF16),
            pltpu.VMEM((CHUNKS, 2, 128, 512), BF16),
            pltpu.VMEM((CHUNKS, 2, 128, 512), F32),
            pltpu.VMEM((CHUNKS, NX, 2, 32, 512), BF16),
            pltpu.VMEM((CHUNKS, 6, 32, 512), BF16),
            pltpu.VMEM((CHUNKS, 2, 2, 16, 512), F32),
            pltpu.VMEM((CHUNKS, 2, 16, 512), BF16),
            pltpu.VMEM((CHUNKS, 2, 16, 512), BF16),
            pltpu.VMEM((PLANES, 2, 16, 512), BF16),
            pltpu.VMEM((PLANES, 2, 16, 512), BF16),
            pltpu.VMEM((NZ, 2, 16, 512), F32),
            pltpu.VMEM((16, 512), F32),
            dma((11,)),
            dma((SLOTS, PARTS)),
            dma((2, SLOTS)),
            dma((4,)),
            dma((8, 4)),
            dma((5,)),
            dma((3,)),
            dma((3,)),
            dma((3,)),
            dma((3,)),
            dma((3,)),
            dma((3,)),
            dma((2,)),
            dma((2,)),
            dma((CHUNKS,)),
            dma((1,)),
            dma((CHUNKS, 6)),
            dma((6,)),
            dma((CHUNKS,)),
            dma((1,)),
            dma((PLANES,)),
            dma((1,)),
        ],
        compiler_params=pltpu.CompilerParams(
            collective_id=0, has_side_effects=True, vmem_limit_bytes=60 * 1024 * 1024
        ),
        name="attention_input_grad",
    )(hidden, norm_gain.reshape(1, D), w_query, w_key.T, w_value.T, grad_context, *tables)


def solution(mesh):
    in_specs = (
        P("dp", None),
        P(),
        P("dp", "tensor"),
        P("dp", "tensor"),
        P("dp", "tensor"),
        P("dp", "tensor"),
    )
    out_specs = P(("dp", "tensor"), None)
    return jax.shard_map(
        per_device, mesh=mesh, in_specs=in_specs, out_specs=out_specs, check_vma=False
    )
```

```python
import functools
import math

import jax
import jax.numpy as jnp
import numpy as np
from jax import lax
from jax.experimental import pallas as pl
from jax.experimental.pallas import tpu as pltpu
from jax.sharding import PartitionSpec as P

D = 8192
HD = 128
SEQ = 256
NZ, NY, NX = 8, 4, 4
PLANES = NZ // 2
SLOTS = PLANES * NY
ROWS = 640
PARTS = 4
PART = ROWS // PARTS
LAG_B, LAG_C = 2, 4
PAIR_STEP, SPREAD_STEP, PARTNER_STEP, PARTNER_PLANES = 4, 8, 9, 4
WORD_STEPS = (3, 5, 7, 10)
CHUNKS = 8
LAG_X, LAG_O = 2, 3
ROPE_THETA = 500000.0
SCALE = 1.0 / math.sqrt(HD)
MESH = pl.DeviceIdType.MESH
F32, BF16 = jnp.float32, jnp.bfloat16


def rotary_tables():
    lane = np.arange(HD)
    frequency = np.exp((lane // 2) * (-2.0 * math.log(ROPE_THETA) / HD))
    angle = np.arange(SEQ)[:, None] * frequency[None, :]
    cosine = np.cos(angle)
    sine = np.sin(angle) * np.where(lane % 2 == 0, -1.0, 1.0)[None, :]
    packed_cos = np.ones((4, 128, 128))
    packed_sin = np.zeros((4, 128, 128))
    for rank in range(4):
        columns = slice(32 * rank, 32 * rank + 32)
        for part in range(2):
            rows = slice(128 * part, 128 * part + 128)
            packed_cos[rank, :, 64 * part : 64 * part + 32] = cosine[rows, columns]
            packed_sin[rank, :, 64 * part : 64 * part + 32] = sine[rows, columns]
    return [table.astype(np.float32) for table in (cosine, sine, packed_cos, packed_sin)]


def dot(left, right):
    return lax.dot_general(left, right, (((1,), (0,)), ((), ())), preferred_element_type=F32)


def dot_rows(left, right):
    return lax.dot_general(left, right, (((1,), (1,)), ((), ())), preferred_element_type=F32)


def dot_columns(left, right):
    return lax.dot_general(left, right, (((0,), (0,)), ((), ())), preferred_element_type=F32)


def lanes_of(value):
    return lax.broadcasted_iota(jnp.int32, value.shape, 1)


def rotate(value, cosine, sine):
    left = pltpu.roll(value, 127, 1)
    right = pltpu.roll(value, 1, 1)
    swapped = jnp.where(lanes_of(value) % 2 == 0, left, right)
    return value * cosine + swapped * sine


def kernel(
    hid_hbm, gain_hbm, wq_hbm, wk_hbm, wv_hbm, gc_hbm, cos_hbm, sin_hbm, kcos_hbm, ksin_hbm,
    out_ref,
    hid, gain, wkv, gc, cosine, sine, kcos, ksin, W, N, given, qacc, kvacc, qs, qr, ks, kr,
    kvs, dks, dkr, AQ, AK, dkvs, T, sibs, sibr, own, S, xin, fs, zsend, zin, ps, pr, G, dots,
    word, load_sem, ag_recv, ag_send, ag_sent, n_recv, n_sent, q_recv, q_send, kv_recv, kv_send, dk_recv, dk_send,
    a_recv, a_send, sib_recv, sib_send, x_recv, x_send, z_recv, z_send, p_recv, p_send,
):
    dp = lax.axis_index("dp")
    tensor = lax.axis_index("tensor")
    z, y = dp // NY, dp % NY
    side, zz = z % 2, z // 2
    zh, x, c = tensor // 8, (tensor // 2) % NX, tensor % 2
    rank = tensor % 4
    share = tensor % 8
    yl, yr, yo = (y + 3) % 4, (y + 1) % 4, (y + 2) % 4
    xl, xr, xo = (x + 3) % 4, (x + 1) % 4, (x + 2) % 4

    def at_dp(zz, yy):
        return (zz * NY + yy, tensor)

    def at_tensor(zhh, xx, cc):
        return (dp, zhh * 8 + xx * 2 + cc)

    up, down = at_dp(z + 2, y), at_dp(z - 2, y)
    pair = at_dp(z + 1 - 2 * side, y)
    to_yl, to_yr = at_dp(z, yl), at_dp(z, yr)
    to_xl, to_xr, to_xo = at_tensor(zh, xl, c), at_tensor(zh, xr, c), at_tensor(zh, xo, c)
    sibling = at_tensor(zh, x, 1 - c)
    far = at_tensor(1 - zh, x, c)
    x_pair = x + 1 - 2 * (x % 2)
    group = {1: sibling, 2: at_tensor(zh, x_pair, c), 3: at_tensor(zh, x_pair, 1 - c)}

    def remote(src, dst, send, recv, device):
        return pltpu.make_async_remote_copy(
            src_ref=src, dst_ref=dst, send_sem=send, recv_sem=recv, device_id=device, device_id_type=MESH
        )

    def plane_start(j, which):
        return (2 * j + which) * 1024

    mine = zz * NY + y

    def load(k, src, dst):
        return pltpu.make_async_copy(src, dst, load_sem.at[k])

    load_weights = [
        load(0, wq_hbm.at[:, pl.ds(0, 128)], W.at[mine, pl.ds(0, 256)]),
        load(1, wq_hbm.at[:, pl.ds(128, 128)], W.at[mine, pl.ds(256, 256)]),
        load(2, wk_hbm, wkv.at[0]),
        load(3, wv_hbm, wkv.at[1]),
    ]
    load_rows = [load(4, hid_hbm, hid), load(5, gain_hbm, gain)]
    load_rest = [
        load(6, gc_hbm, gc),
        load(7, cos_hbm, cosine),
        load(8, sin_hbm, sine),
        load(9, kcos_hbm.at[rank], kcos),
        load(10, ksin_hbm.at[rank], ksin),
    ]
    for copy in load_weights:
        copy.start()
    barrier = pltpu.get_barrier_semaphore()

    def greet(device):
        pl.semaphore_signal(barrier, inc=1, device_id=device, device_id_type=MESH)

    def two_planes(step):
        there = z + step
        other = jnp.where(jnp.logical_and(there >= 0, there < NZ), zh, 1 - zh)
        return ((there + NZ) % NZ * NY + y, other * 8 + share)

    ring_up, ring_down = two_planes(2), two_planes(-2)
    for device in (to_yl, to_yr, to_xl, to_xr, to_xo, sibling, group[3], pair, ring_up, ring_down):
        greet(device)

    for copy in load_rows + load_rest:
        copy.start()
    for copy in load_weights:
        copy.wait()
    wk, wv = wkv[0].astype(F32), wkv[1].astype(F32)
    packed = jnp.concatenate([wk[:, :128], wv[:, :128], wk[:, 128:], wv[:, 128:]], axis=0)
    W[mine, 512:640, :] = packed.T.astype(BF16)
    pl.semaphore_wait(barrier, 10)

    def pass_word(k):
        pl.semaphore_signal(word.at[k], inc=1, device_id=ring_up, device_id_type=MESH)

    pass_word(0)

    def block(i, p, device, kind):
        rows = pl.ds(p * PART, PART)
        if kind in (0, 4):
            send = ag_send.at[kind // 4, i]
        elif kind == 3:
            send = ag_sent.at[2 + p // (PARTS // 2)]
        else:
            send = ag_sent.at[kind - 1]
        return remote(W.at[i, rows], W.at[i, rows], send, ag_recv.at[i, p], device)

    def sent(src, send, device):
        return remote(src, src, send, ag_recv.at[0, 0], device)

    def plane(n):
        s = (n + 1) // 2
        return jnp.where(n % 2 == 1, zz - s, zz + s)

    def inside(j):
        return jnp.logical_and(j >= 0, j < PLANES)

    def go_up(j):
        return jnp.logical_and(j <= zz, zz < PLANES - 1)

    def go_down(j):
        return jnp.logical_and(j >= zz, zz > 0)

    def spread(j, p):
        i = j * NY + y

        @pl.when(go_up(j))
        def _():
            block(i, p, up, 0).start()

        @pl.when(go_down(j))
        def _():
            block(i, p, down, 4).start()

        block(i, p, to_yr, 1).start()
        block(i, p, to_yl, 2).start()

    def rows_of(which, i):
        return N[which, i // 2, :, pl.ds(pl.multiple_of((i % 2) * 256, 256), 256)]

    def multiply_q(which, i):
        rows = rows_of(which, i)
        qacc[which, 0] += dot(rows, W[i, 0:256, :])
        qacc[which, 1] += dot(rows, W[i, 256:512, :])

    def multiply_kv(which, i):
        rows = rows_of(which, i)
        both = W[i, 512:640, :]
        kvacc[which, 0] += dot(rows[:, 0:128], both)
        kvacc[which, 1] += dot(rows[:, 128:256], both)

    def multiply(i):
        multiply_q(0, i)
        multiply_kv(0, i)

    for p in range(PARTS):
        spread(zz, p)
    qacc[...] = jnp.zeros_like(qacc)
    kvacc[...] = jnp.zeros_like(kvacc)

    given_start = pl.multiple_of(plane_start(share // 2, 1 - side) + (share % 2) * 512, 512)

    def norm_rows(b):
        rows = pl.ds(pl.multiple_of(b * 16, 16), 16)
        values = hid[rows, :].astype(F32)
        inverse = lax.rsqrt(jnp.mean(values * values, axis=1, keepdims=True) + 1e-05)

        def normed(start):
            columns = pl.ds(start, 512)
            return (hid[rows, columns].astype(F32) * inverse * gain[:, columns]).astype(BF16)

        given[rows, :] = normed(given_start)
        for e in range(8):
            start = pl.multiple_of(plane_start(e // 2, side) + (e % 2) * 512, 512)
            N[0, e, rows, :] = normed(start)

    def quarter(r):
        return pl.ds(pl.multiple_of(r * 64, 64), 64)

    def give(r):
        return remote(given.at[quarter(r)], N.at[1, share, quarter(r)], n_sent.at[0], n_recv.at[share, r], pair)

    def hand(kind, e, r, device):
        ref = N.at[1, e, quarter(r)]
        return remote(ref, ref, n_sent.at[kind], n_recv.at[e, r], device)

    for copy in load_rows:
        copy.wait()

    def norm_step(r, carry):
        def inner(b, inside_carry):
            norm_rows(r * 4 + b)
            return inside_carry

        lax.fori_loop(0, 4, inner, 0)
        give(r).start()
        return carry

    lax.fori_loop(0, 4, norm_step, 0)

    def spread_given(r, carry):
        give(r).wait_recv()
        hand(1, share, r, to_xr).start()
        hand(2, share, r, to_xl).start()
        hand(3, share, r, to_xo).start()
        hand(4, share, r, sibling).start()
        return carry

    def pass_given(r, carry):
        for xx, device in ((xl, to_xr), (xr, to_xl), (xo, to_xo)):
            e = xx * 2 + c
            hand(1, e, r, device).wait_recv()
            hand(4, e, r, sibling).start()
        return carry

    def wait_given(r, carry):
        for xx in range(NX):
            hand(4, xx * 2 + 1 - c, r, sibling).wait_recv()
        return carry

    def partner_planes(product, first, last):
        def step(n, carry):
            j = plane(n)

            @pl.when(inside(j))
            def _():
                for k in range(NY):
                    product(1, j * NY + k)

            return carry

        lax.fori_loop(first, last, step, 0)

    def gather_step(n, carry):
        for k in range(4):

            @pl.when(n == WORD_STEPS[k])
            def _(k=k):
                pl.semaphore_wait(word.at[k], 1)
                if k < 3:
                    pass_word(k + 1)

        @pl.when(n == PAIR_STEP)
        def _():
            lax.fori_loop(0, 4, spread_given, 0)

        @pl.when(n == SPREAD_STEP)
        def _():
            lax.fori_loop(0, 4, pass_given, 0)

        ja = plane(n)

        @pl.when(jnp.logical_and(inside(ja), n < 2 * PLANES - 1))
        def _():
            i = ja * NY + y
            for p in range(PARTS):
                block(i, p, up, 0).wait_recv()
                spread(ja, p)

        jb = plane(n - LAG_B)

        @pl.when(jnp.logical_and(inside(jb), jnp.logical_and(n >= LAG_B, n < 2 * PLANES - 1 + LAG_B)))
        def _():
            i_left, i_right = jb * NY + yl, jb * NY + yr
            for p in range(PARTS):
                block(i_left, p, to_yr, 1).wait_recv()
                if p < PARTS // 2:
                    block(i_left, p, to_yr, 3).start()
                block(i_right, p, to_yl, 2).wait_recv()
                if p >= PARTS // 2:
                    block(i_right, p, to_yl, 3).start()
            multiply(jb * NY + y)
            multiply(i_left)
            multiply(i_right)

        jc = plane(n - LAG_C)

        @pl.when(jnp.logical_and(inside(jc), n >= LAG_C))
        def _():
            i = jc * NY + yo
            for p in range(PARTS):
                block(i, p, to_yr, 3).wait_recv()
            multiply(i)

        @pl.when(n == PARTNER_STEP)
        def _():
            lax.fori_loop(0, 4, wait_given, 0)
            partner_planes(multiply_q, 0, PARTNER_PLANES)
            partner_planes(multiply_kv, 0, PARTNER_PLANES)

        return carry

    lax.fori_loop(1, 2 * PLANES - 1 + LAG_C, gather_step, 0)

    for copy in load_rest:
        copy.wait()

    def gather_sent():
        def chain_sent(j, carry):
            i = j * NY + y

            @pl.when(go_up(j))
            def _():
                sent(W.at[i], ag_send.at[0, i], up).wait_send()

            @pl.when(go_down(j))
            def _():
                sent(W.at[i], ag_send.at[1, i], down).wait_send()

            return carry

        lax.fori_loop(0, PLANES, chain_sent, 0)
        all_blocks, all_halves = W.at[pl.ds(0, PLANES)], W.at[pl.ds(0, PLANES), pl.ds(0, ROWS // 2)]
        sent(all_blocks, ag_sent.at[0], to_yr).wait_send()
        sent(all_blocks, ag_sent.at[1], to_yl).wait_send()
        sent(all_halves, ag_sent.at[2], to_yr).wait_send()
        sent(all_halves, ag_sent.at[3], to_yl).wait_send()
        sent(given, n_sent.at[0], pair).wait_send()
        for kind, device in ((1, to_xr), (2, to_xl), (3, to_xo)):
            sent(given, n_sent.at[kind], device).wait_send()
        sent(N.at[1, pl.ds(0, 4)], n_sent.at[4], sibling).wait_send()

    lane = lax.broadcasted_iota(jnp.int32, (128, 128), 1)

    def pack_kv(which):
        kva, kvb = kvacc[which, 0], kvacc[which, 1]
        low = kva[:128] + pltpu.roll(kvb[:128], 64, 1)
        high = pltpu.roll(kva[128:], 64, 1) + kvb[128:]
        return jnp.where(lane < 64, low, high)

    def ks_copy():
        return remote(ks, kr, q_send.at[0], q_recv.at[0], pair)

    def qs_copy(h):
        return remote(qs.at[h], qr.at[h], q_send.at[1 + h], q_recv.at[1 + h], pair)

    partner_planes(multiply_kv, PARTNER_PLANES, 2 * PLANES - 1)
    ks[...] = pack_kv(1).astype(BF16)
    ks_copy().start()
    partner_planes(multiply_q, PARTNER_PLANES, 2 * PLANES - 1)
    for h in range(2):
        qs[h] = qacc[1, h].astype(BF16)
        qs_copy(h).start()

    kv_mine = pack_kv(0)
    gather_sent()
    ks_copy().wait()
    kv_own = rotate(kv_mine + kr[...].astype(F32), kcos[...], ksin[...])
    kvs[rank] = kv_own.astype(BF16)

    def peer(step):
        if step == 1:
            return rank + 1 - 2 * (rank % 2)
        if step == 2:
            return (rank + 2) % 4
        return 3 - rank

    def kv_copy(step):
        return remote(kvs.at[rank], kvs.at[rank], kv_send.at[step - 1], kv_recv.at[step - 1], group[step])

    for step in (1, 2, 3):
        kv_copy(step).start()
    q_heads = []
    for h in range(2):
        qs_copy(h).wait()
        q_sum = qacc[0, h] + qr[h].astype(F32)
        q_heads.append(rotate(q_sum, cosine[...], sine[...]).astype(BF16))
    for step in (1, 2, 3):
        kv_copy(step).wait()

    def unpack(shift):
        parts = []
        for part in range(2):
            total = jnp.zeros((128, 128), F32)
            for r in range(4):
                piece = kvs[r].astype(F32)
                amount = (32 * r - shift - 64 * part) % 128
                piece = pltpu.roll(piece, amount, 1) if amount else piece
                total = jnp.where(lane // 32 == r, piece, total)
            parts.append(total)
        return jnp.concatenate(parts, axis=0).astype(BF16)

    k_head, v_head = unpack(0), unpack(32)
    row_id = lax.broadcasted_iota(jnp.int32, (SEQ, SEQ), 0)
    col_id = lax.broadcasted_iota(jnp.int32, (SEQ, SEQ), 1)
    causal = row_id >= col_id
    dk = jnp.zeros((SEQ, HD), F32)
    dv = jnp.zeros((SEQ, HD), F32)
    dq_heads = []
    for h in range(2):
        g_head = gc[:, h * HD : (h + 1) * HD]
        scores = jnp.where(causal, dot_rows(q_heads[h], k_head) * SCALE, -1e30)
        weights = jnp.exp(scores - jnp.max(scores, axis=1, keepdims=True))
        probs = weights / jnp.sum(weights, axis=1, keepdims=True)
        grad_probs = dot_rows(g_head, v_head)
        delta = jnp.sum(probs * grad_probs, axis=1, keepdims=True)
        grad_scores = (probs * (grad_probs - delta) * SCALE).astype(BF16)
        dq = dot(grad_scores, k_head)
        dq_heads.append(rotate(dq, cosine[...], -sine[...]).astype(BF16))
        dk = dk + dot_columns(grad_scores, q_heads[h])
        dv = dv + dot_columns(probs.astype(BF16), g_head)

    def pack(r):
        def shifted(value, amount):
            amount = amount % 128
            return pltpu.roll(value, amount, 1) if amount else value

        total = shifted(dk[:128], -32 * r)
        total = jnp.where(lane // 32 == 1, shifted(dv[:128], 32 - 32 * r), total)
        total = jnp.where(lane // 32 == 2, shifted(dk[128:], 64 - 32 * r), total)
        return jnp.where(lane // 32 == 3, shifted(dv[128:], 96 - 32 * r), total)

    for r in range(4):
        dks[r] = pack(r)
    for step in (1, 2, 3):
        dkr[step - 1] = dks[peer(step)].astype(BF16)

    def dk_copy(step):
        return remote(dkr.at[step - 1], dkr.at[step + 2], dk_send.at[step - 1], dk_recv.at[step - 1], group[step])

    for step in (1, 2, 3):
        dk_copy(step).start()

    def ordered(value, core):
        return jnp.concatenate(
            [value[16 * (8 * b + 2 * a + core) : 16 * (8 * b + 2 * a + core) + 16] for a in range(NX) for b in range(2)],
            axis=0,
        )

    def place(ref, value):
        for core in range(2):
            start = pl.multiple_of(jnp.where(c == core, 128, 0), 128)
            ref[pl.ds(start, 128), :] = ordered(value, core)

    def place_kv(which, value):
        turned = pltpu.roll(value, 64, 1)
        first = jnp.concatenate([jnp.where(lane < 64, value, 0.0), jnp.where(lane < 64, turned, 0.0)], axis=0)
        second = jnp.concatenate([jnp.where(lane < 64, 0.0, turned), jnp.where(lane < 64, 0.0, value)], axis=0)
        place(AK.at[which, 0], first.astype(BF16))
        place(AK.at[which, 1], second.astype(BF16))

    def aq_copy():
        return remote(AQ.at[0], AQ.at[1], a_send.at[0], a_recv.at[0], pair)

    def ak_copy():
        return remote(dkvs.at[0], dkvs.at[1], a_send.at[1], a_recv.at[1], pair)

    place(AQ.at[0], jnp.concatenate(dq_heads, axis=1))
    aq_copy().start()

    def weights_q(i):
        return jnp.concatenate([W[i, 0:256, :], W[i, 256:512, :]], axis=1)

    def query_term(j, carry):
        dq = AQ[0]
        for k in range(NY):
            T[j, k] = dot_rows(dq, weights_q(j * NY + k))
        return carry

    lax.fori_loop(0, PLANES, query_term, 0)
    for step in (1, 2, 3):
        dk_copy(step).wait()
    dkv = dks[rank] + dkr[3].astype(F32) + dkr[4].astype(F32) + dkr[5].astype(F32)
    dkv = rotate(dkv, kcos[...], -ksin[...]).astype(BF16)
    dkvs[0] = dkv
    ak_copy().start()
    place_kv(0, dkv.astype(F32))

    def sib_copy(m):
        return remote(sibs.at[m], sibr.at[m], sib_send.at[0], sib_recv.at[m], sibling)

    def x_copy(kind, m):
        x_dst, h, device = ((xo, 0, to_xr), (xo, 1, to_xl), (xr, 1, to_xr), (xl, 0, to_xl), (xr, 0, to_xr), (xl, 1, to_xl))[kind]
        return remote(S.at[m, x_dst, h], xin.at[m, kind], x_send.at[kind], x_recv.at[m, kind], device)

    def far_copy(m):
        return remote(zsend.at[m], zin.at[m], z_send.at[0], z_recv.at[m], far)

    def chunk(m):
        partner = jnp.logical_and(m >= 2, m < 6)
        return partner, jnp.where(m < 2, m, jnp.where(m < 6, m - 2, m - 4))

    def term(m):
        partner, j = chunk(m)

        def add_term(which):
            dkv_a, dkv_b = AK[which, 0], AK[which, 1]
            for k in range(NY):
                i = j * NY + k
                both = W[i, 512:640, :]
                base = T[j, k] if which == 0 else dot_rows(AQ[1], weights_q(i))
                value = base + jnp.concatenate([dot_rows(dkv_a, both), dot_rows(dkv_b, both)], axis=1)
                columns = slice((k % 2) * 256, (k % 2) * 256 + 256)
                sibs[m, k // 2, :, columns] = value[:128].astype(BF16)
                own[m, k // 2, :, columns] = value[128:]

        @pl.when(jnp.logical_not(partner))
        def _():
            add_term(0)

        @pl.when(partner)
        def _():
            add_term(1)

        sib_copy(m).start()

    def over_cores(m):
        sib_copy(m).wait_recv()
        for h in range(2):
            for a in range(NX):
                rows = slice(32 * a, 32 * a + 32)
                S[m, a, h] = (own[m, h, rows, :] + sibr[m, h, rows, :].astype(F32)).astype(BF16)

        for kind in (0, 1, 2, 3):
            x_copy(kind, m).start()

    def over_x(m):
        x_copy(0, m).wait_recv()
        S[m, xr, 0] = (S[m, xr, 0].astype(F32) + xin[m, 0].astype(F32)).astype(BF16)
        x_copy(4, m).start()
        x_copy(1, m).wait_recv()
        S[m, xl, 1] = (S[m, xl, 1].astype(F32) + xin[m, 1].astype(F32)).astype(BF16)
        x_copy(5, m).start()

    def send_far(m, totals):
        for h in range(2):
            fs[m, 0, h] = totals[h][0:16]
            fs[m, 1, h] = totals[h][16:32]
        zsend[m] = fs[m, 1 - zh].astype(BF16)
        far_copy(m).start()

    def at_owner_x(m):
        for kind in (2, 3, 4, 5):
            x_copy(kind, m).wait_recv()
        totals = [
            S[m, x, 0].astype(F32) + xin[m, 3].astype(F32) + xin[m, 4].astype(F32),
            S[m, x, 1].astype(F32) + xin[m, 2].astype(F32) + xin[m, 5].astype(F32),
        ]
        send_far(m, totals)

    own_rows = pl.ds(pl.multiple_of(tensor * 16, 16), 16)

    def pair_copy(j):
        return remote(ps.at[j], pr.at[j], p_send.at[0], p_recv.at[j], pair)

    def scale_plane(j, which, h, value, dots):
        columns = pl.ds(pl.multiple_of(plane_start(j, which) + h * 512, 512), 512)
        scaled = value * gain[:, columns]
        G[2 * j + which, h] = scaled
        dots[...] += scaled * hid[own_rows, columns].astype(F32)

    def at_owner(m, carry):
        partner, j = chunk(m)
        far_copy(m).wait_recv()

        @pl.when(jnp.logical_not(partner))
        def _():
            for h in range(2):
                scale_plane(j, side, h, fs[m, zh, h] + zin[m, h].astype(F32), dots)

        @pl.when(partner)
        def _():
            ps[j] = (fs[m, zh] + zin[m].astype(F32)).astype(BF16)
            pair_copy(j).start()

        return carry

    def from_partner(j, carry):
        pair_copy(j).wait_recv()
        for h in range(2):
            scale_plane(j, 1 - side, h, pr[j, h].astype(F32), dots)
        return carry

    dots[...] = jnp.zeros_like(dots)

    def sum_step(n, carry):
        @pl.when(n == 2)
        def _():
            aq_copy().wait()
            ak_copy().wait()
            place_kv(1, dkvs[1].astype(F32))

        @pl.when(n < CHUNKS)
        def _():
            term(n)

        @pl.when(jnp.logical_and(n >= 1, n < CHUNKS + 1))
        def _():
            over_cores(n - 1)

        @pl.when(jnp.logical_and(n >= LAG_X, n < CHUNKS + LAG_X))
        def _():
            over_x(n - LAG_X)

        @pl.when(n >= LAG_O)
        def _():
            at_owner_x(n - LAG_O)

        return carry

    lax.fori_loop(0, CHUNKS + LAG_O, sum_step, 0)

    remote(sibs, sibr, sib_send.at[0], sib_recv.at[0], sibling).wait_send()
    for kind in range(6):
        x_dst = (to_xr, to_xl)[kind % 2]
        remote(S.at[:, 0, 0], xin.at[:, 0], x_send.at[kind], x_recv.at[0, 0], x_dst).wait_send()
    lax.fori_loop(0, 6, at_owner, 0)
    lax.fori_loop(0, PLANES, from_partner, 0)
    lax.fori_loop(6, CHUNKS, at_owner, 0)
    mean_term = jnp.sum(dots[...], axis=1, keepdims=True) * (1.0 / D)
    own_hidden = hid[own_rows, :].astype(F32)
    inverse = lax.rsqrt(jnp.mean(own_hidden * own_hidden, axis=1, keepdims=True) + 1e-05)
    factor = inverse * inverse * mean_term
    for m in range(NZ):
        for h in range(2):
            columns = slice(m * 1024 + h * 512, m * 1024 + h * 512 + 512)
            value = inverse * (G[m, h] - own_hidden[:, columns] * factor)
            out_ref[:, columns] = value.astype(BF16)

    remote(zsend, zin, z_send.at[0], z_recv.at[0], far).wait_send()
    remote(ps, pr, p_send.at[0], p_recv.at[0], pair).wait_send()


def per_device(hidden, norm_gain, w_query, w_key, w_value, grad_context):
    tables = [jnp.asarray(table) for table in rotary_tables()]
    vmem = pl.BlockSpec(memory_space=pltpu.VMEM)
    hbm = pl.BlockSpec(memory_space=pl.ANY)
    dma = pltpu.SemaphoreType.DMA
    return pl.pallas_call(
        kernel,
        out_shape=jax.ShapeDtypeStruct((16, D), BF16),
        in_specs=[hbm] * 10,
        out_specs=vmem,
        scratch_shapes=[
            pltpu.VMEM((SEQ, D), BF16),
            pltpu.VMEM((1, D), F32),
            pltpu.VMEM((2, 32, 256), BF16),
            pltpu.VMEM((SEQ, 256), BF16),
            pltpu.VMEM((SEQ, HD), F32),
            pltpu.VMEM((SEQ, HD), F32),
            pltpu.VMEM((128, 128), F32),
            pltpu.VMEM((128, 128), F32),
            pltpu.VMEM((SLOTS, ROWS, 128), BF16),
            pltpu.VMEM((2, 8, SEQ, 512), BF16),
            pltpu.VMEM((SEQ, 512), BF16),
            pltpu.VMEM((2, 2, SEQ, HD), F32),
            pltpu.VMEM((2, 2, SEQ, HD), F32),
            pltpu.VMEM((2, SEQ, HD), BF16),
            pltpu.VMEM((2, SEQ, HD), BF16),
            pltpu.VMEM((128, 128), BF16),
            pltpu.VMEM((128, 128), BF16),
            pltpu.VMEM((4, 128, 128), BF16),
            pltpu.VMEM((4, 128, 128), F32),
            pltpu.VMEM((6, 128, 128), BF16),
            pltpu.VMEM((2, SEQ, 256), BF16),
            pltpu.VMEM((2, 2, SEQ, 128), BF16),
            pltpu.VMEM((2, 128, 128), BF16),
            pltpu.VMEM((PLANES, NY, SEQ, 256), F32),
            pltpu.VMEM((CHUNKS, 2, 128, 512), BF16),
            pltpu.VMEM((CHUNKS, 2, 128, 512), BF16),
            pltpu.VMEM((CHUNKS, 2, 128, 512), F32),
            pltpu.VMEM((CHUNKS, NX, 2, 32, 512), BF16),
            pltpu.VMEM((CHUNKS, 6, 32, 512), BF16),
            pltpu.VMEM((CHUNKS, 2, 2, 16, 512), F32),
            pltpu.VMEM((CHUNKS, 2, 16, 512), BF16),
            pltpu.VMEM((CHUNKS, 2, 16, 512), BF16),
            pltpu.VMEM((PLANES, 2, 16, 512), BF16),
            pltpu.VMEM((PLANES, 2, 16, 512), BF16),
            pltpu.VMEM((NZ, 2, 16, 512), F32),
            pltpu.VMEM((16, 512), F32),
            pltpu.SemaphoreType.REGULAR((4,)),
            dma((11,)),
            dma((SLOTS, PARTS)),
            dma((2, SLOTS)),
            dma((4,)),
            dma((8, 4)),
            dma((5,)),
            dma((3,)),
            dma((3,)),
            dma((3,)),
            dma((3,)),
            dma((3,)),
            dma((3,)),
            dma((2,)),
            dma((2,)),
            dma((CHUNKS,)),
            dma((1,)),
            dma((CHUNKS, 6)),
            dma((6,)),
            dma((CHUNKS,)),
            dma((1,)),
            dma((PLANES,)),
            dma((1,)),
        ],
        compiler_params=pltpu.CompilerParams(
            collective_id=0, has_side_effects=True, vmem_limit_bytes=60 * 1024 * 1024
        ),
        name="attention_input_grad",
    )(hidden, norm_gain.reshape(1, D), w_query, w_key.T, w_value.T, grad_context, *tables)


def solution(mesh):
    in_specs = (
        P("dp", None),
        P(),
        P("dp", "tensor"),
        P("dp", "tensor"),
        P("dp", "tensor"),
        P("dp", "tensor"),
    )
    out_specs = P(("dp", "tensor"), None)
    return jax.shard_map(
        per_device, mesh=mesh, in_specs=in_specs, out_specs=out_specs, check_vma=False
    )
```

```python
import functools
import math

import jax
import jax.numpy as jnp
import numpy as np
from jax import lax
from jax.experimental import pallas as pl
from jax.experimental.pallas import tpu as pltpu
from jax.sharding import PartitionSpec as P

D = 8192
HD = 128
SEQ = 256
NZ, NY, NX = 8, 4, 4
PLANES = NZ // 2
SLOTS = PLANES * NY
ROWS = 640
PARTS = 4
PART = ROWS // PARTS
LAG_B, LAG_C = 2, 4
PAIR_STEP, SPREAD_STEP, PARTNER_STEP, PARTNER_PLANES = 5, 9, 10, 4
WORD_STEPS = (3, 5, 7, 10)
CHUNKS = 8
LAG_X, LAG_O = 2, 3
ROPE_THETA = 500000.0
SCALE = 1.0 / math.sqrt(HD)
MESH = pl.DeviceIdType.MESH
F32, BF16 = jnp.float32, jnp.bfloat16


def rotary_tables():
    lane = np.arange(HD)
    frequency = np.exp((lane // 2) * (-2.0 * math.log(ROPE_THETA) / HD))
    angle = np.arange(SEQ)[:, None] * frequency[None, :]
    cosine = np.cos(angle)
    sine = np.sin(angle) * np.where(lane % 2 == 0, -1.0, 1.0)[None, :]
    packed_cos = np.ones((4, 128, 128))
    packed_sin = np.zeros((4, 128, 128))
    for rank in range(4):
        columns = slice(32 * rank, 32 * rank + 32)
        for part in range(2):
            rows = slice(128 * part, 128 * part + 128)
            packed_cos[rank, :, 64 * part : 64 * part + 32] = cosine[rows, columns]
            packed_sin[rank, :, 64 * part : 64 * part + 32] = sine[rows, columns]
    return [table.astype(np.float32) for table in (cosine, sine, packed_cos, packed_sin)]


def dot(left, right):
    return lax.dot_general(left, right, (((1,), (0,)), ((), ())), preferred_element_type=F32)


def dot_rows(left, right):
    return lax.dot_general(left, right, (((1,), (1,)), ((), ())), preferred_element_type=F32)


def dot_columns(left, right):
    return lax.dot_general(left, right, (((0,), (0,)), ((), ())), preferred_element_type=F32)


def lanes_of(value):
    return lax.broadcasted_iota(jnp.int32, value.shape, 1)


def rotate(value, cosine, sine):
    left = pltpu.roll(value, 127, 1)
    right = pltpu.roll(value, 1, 1)
    swapped = jnp.where(lanes_of(value) % 2 == 0, left, right)
    return value * cosine + swapped * sine


def kernel(
    hid_hbm, gain_hbm, wq_hbm, wk_hbm, wv_hbm, gc_hbm, cos_hbm, sin_hbm, kcos_hbm, ksin_hbm,
    out_ref,
    hid, gain, wkv, gc, cosine, sine, kcos, ksin, W, N, given, qacc, kvacc, qs, qr, ks, kr,
    kvs, dks, dkr, AQ, AK, dkvs, T, sibs, sibr, own, S, xin, fs, zsend, zin, ps, pr, G, dots,
    word, load_sem, ag_recv, ag_send, ag_sent, n_recv, n_sent, q_recv, q_send, kv_recv, kv_send, dk_recv, dk_send,
    a_recv, a_send, sib_recv, sib_send, x_recv, x_send, z_recv, z_send, p_recv, p_send,
):
    dp = lax.axis_index("dp")
    tensor = lax.axis_index("tensor")
    z, y = dp // NY, dp % NY
    side, zz = z % 2, z // 2
    zh, x, c = tensor // 8, (tensor // 2) % NX, tensor % 2
    rank = tensor % 4
    share = tensor % 8
    yl, yr, yo = (y + 3) % 4, (y + 1) % 4, (y + 2) % 4
    xl, xr, xo = (x + 3) % 4, (x + 1) % 4, (x + 2) % 4

    def at_dp(zz, yy):
        return (zz * NY + yy, tensor)

    def at_tensor(zhh, xx, cc):
        return (dp, zhh * 8 + xx * 2 + cc)

    up, down = at_dp(z + 2, y), at_dp(z - 2, y)
    pair = at_dp(z + 1 - 2 * side, y)
    to_yl, to_yr = at_dp(z, yl), at_dp(z, yr)
    to_xl, to_xr, to_xo = at_tensor(zh, xl, c), at_tensor(zh, xr, c), at_tensor(zh, xo, c)
    sibling = at_tensor(zh, x, 1 - c)
    far = at_tensor(1 - zh, x, c)
    far_pair = ((z + 1 - 2 * side) * NY + y, (1 - zh) * 8 + share)
    x_pair = x + 1 - 2 * (x % 2)
    group = {1: sibling, 2: at_tensor(zh, x_pair, c), 3: at_tensor(zh, x_pair, 1 - c)}

    def remote(src, dst, send, recv, device):
        return pltpu.make_async_remote_copy(
            src_ref=src, dst_ref=dst, send_sem=send, recv_sem=recv, device_id=device, device_id_type=MESH
        )

    def plane_start(j, which):
        return (2 * j + which) * 1024

    mine = zz * NY + y

    def load(k, src, dst):
        return pltpu.make_async_copy(src, dst, load_sem.at[k])

    load_weights = [
        load(0, wq_hbm.at[:, pl.ds(0, 128)], W.at[mine, pl.ds(0, 256)]),
        load(1, wq_hbm.at[:, pl.ds(128, 128)], W.at[mine, pl.ds(256, 256)]),
        load(2, wk_hbm, wkv.at[0]),
        load(3, wv_hbm, wkv.at[1]),
    ]
    load_rows = [load(4, hid_hbm, hid), load(5, gain_hbm, gain)]
    load_rest = [
        load(6, gc_hbm, gc),
        load(7, cos_hbm, cosine),
        load(8, sin_hbm, sine),
        load(9, kcos_hbm.at[rank], kcos),
        load(10, ksin_hbm.at[rank], ksin),
    ]
    for copy in load_weights:
        copy.start()
    barrier = pltpu.get_barrier_semaphore()

    def greet(device):
        pl.semaphore_signal(barrier, inc=1, device_id=device, device_id_type=MESH)

    def two_planes(step):
        there = z + step
        other = jnp.where(jnp.logical_and(there >= 0, there < NZ), zh, 1 - zh)
        return ((there + NZ) % NZ * NY + y, other * 8 + share)

    ring_up, ring_down = two_planes(2), two_planes(-2)
    for device in (to_yl, to_yr, to_xl, to_xr, to_xo, sibling, group[3], pair, ring_up, ring_down):
        greet(device)

    for copy in load_rows + load_rest:
        copy.start()
    for copy in load_weights:
        copy.wait()
    wk, wv = wkv[0].astype(F32), wkv[1].astype(F32)
    packed = jnp.concatenate([wk[:, :128], wv[:, :128], wk[:, 128:], wv[:, 128:]], axis=0)
    W[mine, 512:640, :] = packed.T.astype(BF16)
    pl.semaphore_wait(barrier, 10)

    def pass_word(k):
        pl.semaphore_signal(word.at[k], inc=1, device_id=ring_up, device_id_type=MESH)

    pass_word(0)

    def block(i, p, device, kind):
        rows = pl.ds(p * PART, PART)
        if kind in (0, 4):
            send = ag_send.at[kind // 4, i]
        elif kind == 3:
            send = ag_sent.at[2 + p // (PARTS // 2)]
        else:
            send = ag_sent.at[kind - 1]
        return remote(W.at[i, rows], W.at[i, rows], send, ag_recv.at[i, p], device)

    def sent(src, send, device):
        return remote(src, src, send, ag_recv.at[0, 0], device)

    def plane(n):
        s = (n + 1) // 2
        return jnp.where(n % 2 == 1, zz - s, zz + s)

    def inside(j):
        return jnp.logical_and(j >= 0, j < PLANES)

    def go_up(j):
        return jnp.logical_and(j <= zz, zz < PLANES - 1)

    def go_down(j):
        return jnp.logical_and(j >= zz, zz > 0)

    def spread(j, p):
        i = j * NY + y

        @pl.when(go_up(j))
        def _():
            block(i, p, up, 0).start()

        @pl.when(go_down(j))
        def _():
            block(i, p, down, 4).start()

        block(i, p, to_yr, 1).start()
        block(i, p, to_yl, 2).start()

    def rows_of(which, i):
        return N[which, i // 2, :, pl.ds(pl.multiple_of((i % 2) * 256, 256), 256)]

    def multiply_q(which, i):
        rows = rows_of(which, i)
        qacc[which, 0] += dot(rows, W[i, 0:256, :])
        qacc[which, 1] += dot(rows, W[i, 256:512, :])

    def multiply_kv(which, i):
        rows = rows_of(which, i)
        both = W[i, 512:640, :]
        kvacc[which, 0] += dot(rows[:, 0:128], both)
        kvacc[which, 1] += dot(rows[:, 128:256], both)

    def multiply(i):
        multiply_q(0, i)
        multiply_kv(0, i)

    for p in range(PARTS):
        spread(zz, p)
    qacc[...] = jnp.zeros_like(qacc)
    kvacc[...] = jnp.zeros_like(kvacc)

    given_start = pl.multiple_of(plane_start(share // 2, 1 - side) + (share % 2) * 512, 512)

    def norm_rows(b):
        rows = pl.ds(pl.multiple_of(b * 16, 16), 16)
        values = hid[rows, :].astype(F32)
        inverse = lax.rsqrt(jnp.mean(values * values, axis=1, keepdims=True) + 1e-05)

        def normed(start):
            columns = pl.ds(start, 512)
            return (hid[rows, columns].astype(F32) * inverse * gain[:, columns]).astype(BF16)

        given[rows, :] = normed(given_start)
        for e in range(8):
            start = pl.multiple_of(plane_start(e // 2, side) + (e % 2) * 512, 512)
            N[0, e, rows, :] = normed(start)

    def quarter(r):
        return pl.ds(pl.multiple_of(r * 64, 64), 64)

    def give(r):
        return remote(given.at[quarter(r)], N.at[1, share, quarter(r)], n_sent.at[0], n_recv.at[share, r], pair)

    def hand(kind, e, r, device):
        ref = N.at[1, e, quarter(r)]
        return remote(ref, ref, n_sent.at[kind], n_recv.at[e, r], device)

    for copy in load_rows:
        copy.wait()

    def norm_step(r, carry):
        def inner(b, inside_carry):
            norm_rows(r * 4 + b)
            return inside_carry

        lax.fori_loop(0, 4, inner, 0)
        return carry

    lax.fori_loop(0, 4, norm_step, 0)

    def spread_given(r, carry):
        give(r).wait_recv()
        hand(1, share, r, to_xr).start()
        hand(2, share, r, to_xl).start()
        hand(3, share, r, to_xo).start()
        hand(4, share, r, sibling).start()
        return carry

    def pass_given(r, carry):
        for xx, device in ((xl, to_xr), (xr, to_xl), (xo, to_xo)):
            e = xx * 2 + c
            hand(1, e, r, device).wait_recv()
            hand(4, e, r, sibling).start()
        return carry

    def wait_given(r, carry):
        for xx in range(NX):
            hand(4, xx * 2 + 1 - c, r, sibling).wait_recv()
        return carry

    def partner_planes(product, first, last):
        def step(n, carry):
            j = plane(n)

            @pl.when(inside(j))
            def _():
                for k in range(NY):
                    product(1, j * NY + k)

            return carry

        lax.fori_loop(first, last, step, 0)

    def gather_step(n, carry):
        for k in range(4):

            @pl.when(n == WORD_STEPS[k])
            def _(k=k):
                pl.semaphore_wait(word.at[k], 1)
                if k < 3:
                    pass_word(k + 1)

        @pl.when(n == PAIR_STEP)
        def _():
            lax.fori_loop(0, 4, spread_given, 0)

        @pl.when(n == SPREAD_STEP)
        def _():
            lax.fori_loop(0, 4, pass_given, 0)

        ja = plane(n)

        @pl.when(jnp.logical_and(inside(ja), n < 2 * PLANES - 1))
        def _():
            i = ja * NY + y
            for p in range(PARTS):
                block(i, p, up, 0).wait_recv()
                spread(ja, p)

        @pl.when(n == 2)
        def _():
            give(0).start()

        @pl.when(n == 2)
        def _():
            give(1).start()

        @pl.when(n == 3)
        def _():
            give(2).start()

        @pl.when(n == 3)
        def _():
            give(3).start()

        jb = plane(n - LAG_B)

        @pl.when(jnp.logical_and(inside(jb), jnp.logical_and(n >= LAG_B, n < 2 * PLANES - 1 + LAG_B)))
        def _():
            i_left, i_right = jb * NY + yl, jb * NY + yr
            for p in range(PARTS):
                block(i_left, p, to_yr, 1).wait_recv()
                if p < PARTS // 2:
                    block(i_left, p, to_yr, 3).start()
                block(i_right, p, to_yl, 2).wait_recv()
                if p >= PARTS // 2:
                    block(i_right, p, to_yl, 3).start()
            multiply(jb * NY + y)
            multiply(i_left)
            multiply(i_right)

        jc = plane(n - LAG_C)

        @pl.when(jnp.logical_and(inside(jc), n >= LAG_C))
        def _():
            i = jc * NY + yo
            for p in range(PARTS):
                block(i, p, to_yr, 3).wait_recv()
            multiply(i)

        @pl.when(n == PARTNER_STEP)
        def _():
            lax.fori_loop(0, 4, wait_given, 0)
            partner_planes(multiply_q, 0, PARTNER_PLANES)
            partner_planes(multiply_kv, 0, PARTNER_PLANES)

        return carry

    lax.fori_loop(1, 2 * PLANES - 1 + LAG_C, gather_step, 0)

    for copy in load_rest:
        copy.wait()

    def gather_sent():
        def chain_sent(j, carry):
            i = j * NY + y

            @pl.when(go_up(j))
            def _():
                sent(W.at[i], ag_send.at[0, i], up).wait_send()

            @pl.when(go_down(j))
            def _():
                sent(W.at[i], ag_send.at[1, i], down).wait_send()

            return carry

        lax.fori_loop(0, PLANES, chain_sent, 0)
        all_blocks, all_halves = W.at[pl.ds(0, PLANES)], W.at[pl.ds(0, PLANES), pl.ds(0, ROWS // 2)]
        sent(all_blocks, ag_sent.at[0], to_yr).wait_send()
        sent(all_blocks, ag_sent.at[1], to_yl).wait_send()
        sent(all_halves, ag_sent.at[2], to_yr).wait_send()
        sent(all_halves, ag_sent.at[3], to_yl).wait_send()
        sent(given, n_sent.at[0], pair).wait_send()
        for kind, device in ((1, to_xr), (2, to_xl), (3, to_xo)):
            sent(given, n_sent.at[kind], device).wait_send()
        sent(N.at[1, pl.ds(0, 4)], n_sent.at[4], sibling).wait_send()

    lane = lax.broadcasted_iota(jnp.int32, (128, 128), 1)

    def pack_kv(which):
        kva, kvb = kvacc[which, 0], kvacc[which, 1]
        low = kva[:128] + pltpu.roll(kvb[:128], 64, 1)
        high = pltpu.roll(kva[128:], 64, 1) + kvb[128:]
        return jnp.where(lane < 64, low, high)

    def ks_copy():
        return remote(ks, kr, q_send.at[0], q_recv.at[0], pair)

    def qs_copy(h):
        return remote(qs.at[h], qr.at[h], q_send.at[1 + h], q_recv.at[1 + h], pair)

    partner_planes(multiply_kv, PARTNER_PLANES, 2 * PLANES - 1)
    ks[...] = pack_kv(1).astype(BF16)
    ks_copy().start()
    partner_planes(multiply_q, PARTNER_PLANES, 2 * PLANES - 1)
    for h in range(2):
        qs[h] = qacc[1, h].astype(BF16)
        qs_copy(h).start()

    kv_mine = pack_kv(0)
    gather_sent()
    ks_copy().wait()
    kv_own = rotate(kv_mine + kr[...].astype(F32), kcos[...], ksin[...])
    kvs[rank] = kv_own.astype(BF16)

    def peer(step):
        if step == 1:
            return rank + 1 - 2 * (rank % 2)
        if step == 2:
            return (rank + 2) % 4
        return 3 - rank

    def kv_copy(step):
        return remote(kvs.at[rank], kvs.at[rank], kv_send.at[step - 1], kv_recv.at[step - 1], group[step])

    for step in (1, 2, 3):
        kv_copy(step).start()
    q_heads = []
    for h in range(2):
        qs_copy(h).wait()
        q_sum = qacc[0, h] + qr[h].astype(F32)
        q_heads.append(rotate(q_sum, cosine[...], sine[...]).astype(BF16))
    for step in (1, 2, 3):
        kv_copy(step).wait()

    def unpack(shift):
        parts = []
        for part in range(2):
            total = jnp.zeros((128, 128), F32)
            for r in range(4):
                piece = kvs[r].astype(F32)
                amount = (32 * r - shift - 64 * part) % 128
                piece = pltpu.roll(piece, amount, 1) if amount else piece
                total = jnp.where(lane // 32 == r, piece, total)
            parts.append(total)
        return jnp.concatenate(parts, axis=0).astype(BF16)

    k_head, v_head = unpack(0), unpack(32)
    row_id = lax.broadcasted_iota(jnp.int32, (SEQ, SEQ), 0)
    col_id = lax.broadcasted_iota(jnp.int32, (SEQ, SEQ), 1)
    causal = row_id >= col_id
    dk = jnp.zeros((SEQ, HD), F32)
    dv = jnp.zeros((SEQ, HD), F32)
    dq_heads = []
    for h in range(2):
        g_head = gc[:, h * HD : (h + 1) * HD]
        scores = jnp.where(causal, dot_rows(q_heads[h], k_head) * SCALE, -1e30)
        weights = jnp.exp(scores - jnp.max(scores, axis=1, keepdims=True))
        probs = weights / jnp.sum(weights, axis=1, keepdims=True)
        grad_probs = dot_rows(g_head, v_head)
        delta = jnp.sum(probs * grad_probs, axis=1, keepdims=True)
        grad_scores = (probs * (grad_probs - delta) * SCALE).astype(BF16)
        dq = dot(grad_scores, k_head)
        dq_heads.append(rotate(dq, cosine[...], -sine[...]).astype(BF16))
        dk = dk + dot_columns(grad_scores, q_heads[h])
        dv = dv + dot_columns(probs.astype(BF16), g_head)

    def pack(r):
        def shifted(value, amount):
            amount = amount % 128
            return pltpu.roll(value, amount, 1) if amount else value

        total = shifted(dk[:128], -32 * r)
        total = jnp.where(lane // 32 == 1, shifted(dv[:128], 32 - 32 * r), total)
        total = jnp.where(lane // 32 == 2, shifted(dk[128:], 64 - 32 * r), total)
        return jnp.where(lane // 32 == 3, shifted(dv[128:], 96 - 32 * r), total)

    for r in range(4):
        dks[r] = pack(r)
    for step in (1, 2, 3):
        dkr[step - 1] = dks[peer(step)].astype(BF16)

    def dk_copy(step):
        return remote(dkr.at[step - 1], dkr.at[step + 2], dk_send.at[step - 1], dk_recv.at[step - 1], group[step])

    for step in (1, 2, 3):
        dk_copy(step).start()

    def ordered(value, core):
        return jnp.concatenate(
            [value[16 * (8 * b + 2 * a + core) : 16 * (8 * b + 2 * a + core) + 16] for a in range(NX) for b in range(2)],
            axis=0,
        )

    def place(ref, value):
        for core in range(2):
            start = pl.multiple_of(jnp.where(c == core, 128, 0), 128)
            ref[pl.ds(start, 128), :] = ordered(value, core)

    def place_kv(which, value):
        turned = pltpu.roll(value, 64, 1)
        first = jnp.concatenate([jnp.where(lane < 64, value, 0.0), jnp.where(lane < 64, turned, 0.0)], axis=0)
        second = jnp.concatenate([jnp.where(lane < 64, 0.0, turned), jnp.where(lane < 64, 0.0, value)], axis=0)
        place(AK.at[which, 0], first.astype(BF16))
        place(AK.at[which, 1], second.astype(BF16))

    def aq_copy():
        return remote(AQ.at[0], AQ.at[1], a_send.at[0], a_recv.at[0], pair)

    def ak_copy():
        return remote(dkvs.at[0], dkvs.at[1], a_send.at[1], a_recv.at[1], pair)

    place(AQ.at[0], jnp.concatenate(dq_heads, axis=1))
    aq_copy().start()

    def weights_q(i):
        return jnp.concatenate([W[i, 0:256, :], W[i, 256:512, :]], axis=1)

    def query_term(j, carry):
        dq = AQ[0]
        for k in range(NY):
            T[j, k] = dot_rows(dq, weights_q(j * NY + k))
        return carry

    lax.fori_loop(0, PLANES, query_term, 0)
    for step in (1, 2, 3):
        dk_copy(step).wait()
    dkv = dks[rank] + dkr[3].astype(F32) + dkr[4].astype(F32) + dkr[5].astype(F32)
    dkv = rotate(dkv, kcos[...], -ksin[...]).astype(BF16)
    dkvs[0] = dkv
    ak_copy().start()
    place_kv(0, dkv.astype(F32))

    def sib_copy(m):
        return remote(sibs.at[m], sibr.at[m], sib_send.at[0], sib_recv.at[m], sibling)

    def x_copy(kind, m):
        x_dst, h, device = ((xo, 0, to_xr), (xo, 1, to_xl), (xr, 1, to_xr), (xl, 0, to_xl), (xr, 0, to_xr), (xl, 1, to_xl))[kind]
        return remote(S.at[m, x_dst, h], xin.at[m, kind], x_send.at[kind], x_recv.at[m, kind], device)

    def far_copy(m, device):
        return remote(zsend.at[m], zin.at[m], z_send.at[0], z_recv.at[m], device)

    def pair_copy(j):
        return remote(ps.at[j], pr.at[j], p_send.at[0], p_recv.at[j], pair)

    def chunk(m):
        partner = jnp.logical_and(m >= 2, m < 6)
        return partner, jnp.where(m < 2, m, jnp.where(m < 6, m - 2, m - 4))

    def term(m):
        partner, j = chunk(m)

        def add_term(which):
            dkv_a, dkv_b = AK[which, 0], AK[which, 1]
            for k in range(NY):
                i = j * NY + k
                both = W[i, 512:640, :]
                base = T[j, k] if which == 0 else dot_rows(AQ[1], weights_q(i))
                value = base + jnp.concatenate([dot_rows(dkv_a, both), dot_rows(dkv_b, both)], axis=1)
                columns = slice((k % 2) * 256, (k % 2) * 256 + 256)
                sibs[m, k // 2, :, columns] = value[:128].astype(BF16)
                own[m, k // 2, :, columns] = value[128:]

        @pl.when(jnp.logical_not(partner))
        def _():
            add_term(0)

        @pl.when(partner)
        def _():
            add_term(1)

        sib_copy(m).start()

    def over_cores(m):
        sib_copy(m).wait_recv()
        for h in range(2):
            for a in range(NX):
                rows = slice(32 * a, 32 * a + 32)
                S[m, a, h] = (own[m, h, rows, :] + sibr[m, h, rows, :].astype(F32)).astype(BF16)

        for kind in (0, 1, 2, 3):
            x_copy(kind, m).start()

    def over_x(m):
        x_copy(0, m).wait_recv()
        S[m, xr, 0] = (S[m, xr, 0].astype(F32) + xin[m, 0].astype(F32)).astype(BF16)
        x_copy(4, m).start()
        x_copy(1, m).wait_recv()
        S[m, xl, 1] = (S[m, xl, 1].astype(F32) + xin[m, 1].astype(F32)).astype(BF16)
        x_copy(5, m).start()

    def send_far(m, totals):
        partner, j = chunk(m)
        for h in range(2):
            fs[m, 0, h] = totals[h][0:16]
            fs[m, 1, h] = totals[h][16:32]
        zsend[m] = fs[m, 1 - zh].astype(BF16)

        @pl.when(jnp.logical_not(partner))
        def _():
            far_copy(m, far).start()

        @pl.when(partner)
        def _():
            far_copy(m, far_pair).start()
            ps[j] = fs[m, zh].astype(BF16)
            pair_copy(j).start()

    def at_owner_x(m):
        for kind in (2, 3, 4, 5):
            x_copy(kind, m).wait_recv()
        totals = [
            S[m, x, 0].astype(F32) + xin[m, 3].astype(F32) + xin[m, 4].astype(F32),
            S[m, x, 1].astype(F32) + xin[m, 2].astype(F32) + xin[m, 5].astype(F32),
        ]
        send_far(m, totals)

    own_rows = pl.ds(pl.multiple_of(tensor * 16, 16), 16)

    def scale_plane(j, which, h, value):
        columns = pl.ds(pl.multiple_of(plane_start(j, which) + h * 512, 512), 512)
        scaled = value * gain[:, columns]
        G[2 * j + which, h] = scaled
        dots[...] += scaled * hid[own_rows, columns].astype(F32)

    def at_owner(m, carry):
        partner, j = chunk(m)
        far_copy(m, far).wait_recv()

        @pl.when(jnp.logical_not(partner))
        def _():
            for h in range(2):
                scale_plane(j, side, h, fs[m, zh, h] + zin[m, h].astype(F32))

        @pl.when(partner)
        def _():
            pair_copy(j).wait_recv()
            for h in range(2):
                scale_plane(j, 1 - side, h, pr[j, h].astype(F32) + zin[m, h].astype(F32))

        return carry

    dots[...] = jnp.zeros_like(dots)

    def sum_step(n, carry):
        @pl.when(n == 2)
        def _():
            aq_copy().wait()
            ak_copy().wait()
            place_kv(1, dkvs[1].astype(F32))

        @pl.when(n < CHUNKS)
        def _():
            term(n)

        @pl.when(jnp.logical_and(n >= 1, n < CHUNKS + 1))
        def _():
            over_cores(n - 1)

        @pl.when(jnp.logical_and(n >= LAG_X, n < CHUNKS + LAG_X))
        def _():
            over_x(n - LAG_X)

        @pl.when(n >= LAG_O)
        def _():
            at_owner_x(n - LAG_O)

        return carry

    lax.fori_loop(0, CHUNKS + LAG_O, sum_step, 0)

    remote(sibs, sibr, sib_send.at[0], sib_recv.at[0], sibling).wait_send()
    for kind in range(6):
        x_dst = (to_xr, to_xl)[kind % 2]
        remote(S.at[:, 0, 0], xin.at[:, 0], x_send.at[kind], x_recv.at[0, 0], x_dst).wait_send()
    lax.fori_loop(0, CHUNKS, at_owner, 0)
    mean_term = jnp.sum(dots[...], axis=1, keepdims=True) * (1.0 / D)
    own_hidden = hid[own_rows, :].astype(F32)
    inverse = lax.rsqrt(jnp.mean(own_hidden * own_hidden, axis=1, keepdims=True) + 1e-05)
    factor = inverse * inverse * mean_term
    for m in range(NZ):
        for h in range(2):
            columns = slice(m * 1024 + h * 512, m * 1024 + h * 512 + 512)
            value = inverse * (G[m, h] - own_hidden[:, columns] * factor)
            out_ref[:, columns] = value.astype(BF16)

    remote(zsend, zin, z_send.at[0], z_recv.at[0], far).wait_send()
    remote(ps, pr, p_send.at[0], p_recv.at[0], pair).wait_send()


def per_device(hidden, norm_gain, w_query, w_key, w_value, grad_context):
    tables = [jnp.asarray(table) for table in rotary_tables()]
    vmem = pl.BlockSpec(memory_space=pltpu.VMEM)
    hbm = pl.BlockSpec(memory_space=pl.ANY)
    dma = pltpu.SemaphoreType.DMA
    return pl.pallas_call(
        kernel,
        out_shape=jax.ShapeDtypeStruct((16, D), BF16),
        in_specs=[hbm] * 10,
        out_specs=vmem,
        scratch_shapes=[
            pltpu.VMEM((SEQ, D), BF16),
            pltpu.VMEM((1, D), F32),
            pltpu.VMEM((2, 32, 256), BF16),
            pltpu.VMEM((SEQ, 256), BF16),
            pltpu.VMEM((SEQ, HD), F32),
            pltpu.VMEM((SEQ, HD), F32),
            pltpu.VMEM((128, 128), F32),
            pltpu.VMEM((128, 128), F32),
            pltpu.VMEM((SLOTS, ROWS, 128), BF16),
            pltpu.VMEM((2, 8, SEQ, 512), BF16),
            pltpu.VMEM((SEQ, 512), BF16),
            pltpu.VMEM((2, 2, SEQ, HD), F32),
            pltpu.VMEM((2, 2, SEQ, HD), F32),
            pltpu.VMEM((2, SEQ, HD), BF16),
            pltpu.VMEM((2, SEQ, HD), BF16),
            pltpu.VMEM((128, 128), BF16),
            pltpu.VMEM((128, 128), BF16),
            pltpu.VMEM((4, 128, 128), BF16),
            pltpu.VMEM((4, 128, 128), F32),
            pltpu.VMEM((6, 128, 128), BF16),
            pltpu.VMEM((2, SEQ, 256), BF16),
            pltpu.VMEM((2, 2, SEQ, 128), BF16),
            pltpu.VMEM((2, 128, 128), BF16),
            pltpu.VMEM((PLANES, NY, SEQ, 256), F32),
            pltpu.VMEM((CHUNKS, 2, 128, 512), BF16),
            pltpu.VMEM((CHUNKS, 2, 128, 512), BF16),
            pltpu.VMEM((CHUNKS, 2, 128, 512), F32),
            pltpu.VMEM((CHUNKS, NX, 2, 32, 512), BF16),
            pltpu.VMEM((CHUNKS, 6, 32, 512), BF16),
            pltpu.VMEM((CHUNKS, 2, 2, 16, 512), F32),
            pltpu.VMEM((CHUNKS, 2, 16, 512), BF16),
            pltpu.VMEM((CHUNKS, 2, 16, 512), BF16),
            pltpu.VMEM((PLANES, 2, 16, 512), BF16),
            pltpu.VMEM((PLANES, 2, 16, 512), BF16),
            pltpu.VMEM((NZ, 2, 16, 512), F32),
            pltpu.VMEM((16, 512), F32),
            pltpu.SemaphoreType.REGULAR((4,)),
            dma((11,)),
            dma((SLOTS, PARTS)),
            dma((2, SLOTS)),
            dma((4,)),
            dma((8, 4)),
            dma((5,)),
            dma((3,)),
            dma((3,)),
            dma((3,)),
            dma((3,)),
            dma((3,)),
            dma((3,)),
            dma((2,)),
            dma((2,)),
            dma((CHUNKS,)),
            dma((1,)),
            dma((CHUNKS, 6)),
            dma((6,)),
            dma((CHUNKS,)),
            dma((1,)),
            dma((PLANES,)),
            dma((1,)),
        ],
        compiler_params=pltpu.CompilerParams(
            collective_id=0, has_side_effects=True, vmem_limit_bytes=60 * 1024 * 1024
        ),
        name="attention_input_grad",
    )(hidden, norm_gain.reshape(1, D), w_query, w_key.T, w_value.T, grad_context, *tables)


def solution(mesh):
    in_specs = (
        P("dp", None),
        P(),
        P("dp", "tensor"),
        P("dp", "tensor"),
        P("dp", "tensor"),
        P("dp", "tensor"),
    )
    out_specs = P(("dp", "tensor"), None)
    return jax.shard_map(
        per_device, mesh=mesh, in_specs=in_specs, out_specs=out_specs, check_vma=False
    )
```

```python
import functools
import math

import jax
import jax.numpy as jnp
import numpy as np
from jax import lax
from jax.experimental import pallas as pl
from jax.experimental.pallas import tpu as pltpu
from jax.sharding import PartitionSpec as P

D = 8192
HD = 128
SEQ = 256
NZ, NY, NX = 8, 4, 4
PLANES = NZ // 2
SLOTS = PLANES * NY
ROWS = 640
PARTS = 4
PART = ROWS // PARTS
LAG_B, LAG_C = 2, 4
PAIR_STEP, SPREAD_STEP, PARTNER_STEP, PARTNER_PLANES = 5, 9, 10, 4
WORD_STEPS = (3, 5, 7, 10)
CHUNKS = 8
LAG_X, LAG_O = 2, 3
ROPE_THETA = 500000.0
SCALE = 1.0 / math.sqrt(HD)
MESH = pl.DeviceIdType.MESH
F32, BF16 = jnp.float32, jnp.bfloat16


def rotary_tables():
    lane = np.arange(HD)
    frequency = np.exp((lane // 2) * (-2.0 * math.log(ROPE_THETA) / HD))
    angle = np.arange(SEQ)[:, None] * frequency[None, :]
    cosine = np.cos(angle)
    sine = np.sin(angle) * np.where(lane % 2 == 0, -1.0, 1.0)[None, :]
    packed_cos = np.ones((4, 128, 128))
    packed_sin = np.zeros((4, 128, 128))
    for rank in range(4):
        columns = slice(32 * rank, 32 * rank + 32)
        for part in range(2):
            rows = slice(128 * part, 128 * part + 128)
            packed_cos[rank, :, 64 * part : 64 * part + 32] = cosine[rows, columns]
            packed_sin[rank, :, 64 * part : 64 * part + 32] = sine[rows, columns]
    return [table.astype(np.float32) for table in (cosine, sine, packed_cos, packed_sin)]


def dot(left, right):
    return lax.dot_general(left, right, (((1,), (0,)), ((), ())), preferred_element_type=F32)


def dot_rows(left, right):
    return lax.dot_general(left, right, (((1,), (1,)), ((), ())), preferred_element_type=F32)


def dot_columns(left, right):
    return lax.dot_general(left, right, (((0,), (0,)), ((), ())), preferred_element_type=F32)


def lanes_of(value):
    return lax.broadcasted_iota(jnp.int32, value.shape, 1)


def rotate(value, cosine, sine):
    left = pltpu.roll(value, 127, 1)
    right = pltpu.roll(value, 1, 1)
    swapped = jnp.where(lanes_of(value) % 2 == 0, left, right)
    return value * cosine + swapped * sine


def kernel(
    hid_hbm, gain_hbm, wq_hbm, wk_hbm, wv_hbm, gc_hbm, cos_hbm, sin_hbm, kcos_hbm, ksin_hbm,
    out_ref,
    hid, gain, wkv, gc, cosine, sine, kcos, ksin, W, N, given, qacc, kvacc, qs, qr, ks, kr,
    kvs, dks, dkr, AQ, AK, dkvs, T, sibs, sibr, own, S, xin, fs, zsend, zin, ps, pr, G, dots,
    word, load_sem, ag_recv, ag_send, ag_sent, n_recv, n_sent, q_recv, q_send, kv_recv, kv_send, dk_recv, dk_send,
    a_recv, a_send, sib_recv, sib_send, x_recv, x_send, z_recv, z_send, p_recv, p_send,
):
    dp = lax.axis_index("dp")
    tensor = lax.axis_index("tensor")
    z, y = dp // NY, dp % NY
    side, zz = z % 2, z // 2
    zh, x, c = tensor // 8, (tensor // 2) % NX, tensor % 2
    rank = tensor % 4
    share = tensor % 8
    yl, yr, yo = (y + 3) % 4, (y + 1) % 4, (y + 2) % 4
    xl, xr, xo = (x + 3) % 4, (x + 1) % 4, (x + 2) % 4

    def at_dp(zz, yy):
        return (zz * NY + yy, tensor)

    def at_tensor(zhh, xx, cc):
        return (dp, zhh * 8 + xx * 2 + cc)

    up, down = at_dp(z + 2, y), at_dp(z - 2, y)
    pair = at_dp(z + 1 - 2 * side, y)
    to_yl, to_yr = at_dp(z, yl), at_dp(z, yr)
    to_xl, to_xr, to_xo = at_tensor(zh, xl, c), at_tensor(zh, xr, c), at_tensor(zh, xo, c)
    sibling = at_tensor(zh, x, 1 - c)
    far = at_tensor(1 - zh, x, c)
    far_pair = ((z + 1 - 2 * side) * NY + y, (1 - zh) * 8 + share)
    x_pair = x + 1 - 2 * (x % 2)
    group = {1: sibling, 2: at_tensor(zh, x_pair, c), 3: at_tensor(zh, x_pair, 1 - c)}

    def remote(src, dst, send, recv, device):
        return pltpu.make_async_remote_copy(
            src_ref=src, dst_ref=dst, send_sem=send, recv_sem=recv, device_id=device, device_id_type=MESH
        )

    def plane_start(j, which):
        return (2 * j + which) * 1024

    mine = zz * NY + y

    def load(k, src, dst):
        return pltpu.make_async_copy(src, dst, load_sem.at[k])

    load_weights = [
        load(0, wq_hbm.at[:, pl.ds(0, 128)], W.at[mine, pl.ds(0, 256)]),
        load(1, wq_hbm.at[:, pl.ds(128, 128)], W.at[mine, pl.ds(256, 256)]),
        load(2, wk_hbm, wkv.at[0]),
        load(3, wv_hbm, wkv.at[1]),
    ]
    load_rows = [load(4, hid_hbm, hid), load(5, gain_hbm, gain)]
    load_rest = [
        load(6, gc_hbm, gc),
        load(7, cos_hbm, cosine),
        load(8, sin_hbm, sine),
        load(9, kcos_hbm.at[rank], kcos),
        load(10, ksin_hbm.at[rank], ksin),
    ]
    for copy in load_weights:
        copy.start()
    barrier = pltpu.get_barrier_semaphore()

    def greet(device):
        pl.semaphore_signal(barrier, inc=1, device_id=device, device_id_type=MESH)

    def two_planes(step):
        there = z + step
        other = jnp.where(jnp.logical_and(there >= 0, there < NZ), zh, 1 - zh)
        return ((there + NZ) % NZ * NY + y, other * 8 + share)

    ring_up, ring_down = two_planes(2), two_planes(-2)
    for device in (to_yl, to_yr, to_xl, to_xr, to_xo, sibling, group[3], pair, ring_up, ring_down):
        greet(device)

    for copy in load_rows + load_rest:
        copy.start()
    for copy in load_weights:
        copy.wait()
    wk, wv = wkv[0].astype(F32), wkv[1].astype(F32)
    packed = jnp.concatenate([wk[:, :128], wv[:, :128], wk[:, 128:], wv[:, 128:]], axis=0)
    W[mine, 512:640, :] = packed.T.astype(BF16)
    pl.semaphore_wait(barrier, 10)

    def pass_word(k):
        pl.semaphore_signal(word.at[k], inc=1, device_id=ring_up, device_id_type=MESH)

    pass_word(0)

    def block(i, p, device, kind):
        rows = pl.ds(p * PART, PART)
        if kind in (0, 4):
            send = ag_send.at[kind // 4, i]
        elif kind == 3:
            send = ag_sent.at[2 + p // (PARTS // 2)]
        else:
            send = ag_sent.at[kind - 1]
        return remote(W.at[i, rows], W.at[i, rows], send, ag_recv.at[i, p], device)

    def sent(src, send, device):
        return remote(src, src, send, ag_recv.at[0, 0], device)

    def plane(n):
        s = (n + 1) // 2
        return jnp.where(n % 2 == 1, zz - s, zz + s)

    def inside(j):
        return jnp.logical_and(j >= 0, j < PLANES)

    def go_up(j):
        return jnp.logical_and(j <= zz, zz < PLANES - 1)

    def go_down(j):
        return jnp.logical_and(j >= zz, zz > 0)

    def spread(j, p):
        i = j * NY + y

        @pl.when(go_up(j))
        def _():
            block(i, p, up, 0).start()

        @pl.when(go_down(j))
        def _():
            block(i, p, down, 4).start()

        block(i, p, to_yr, 1).start()
        block(i, p, to_yl, 2).start()

    def rows_of(which, i):
        return N[which, i // 2, :, pl.ds(pl.multiple_of((i % 2) * 256, 256), 256)]

    def multiply_q(which, i):
        rows = rows_of(which, i)
        qacc[which, 0] += dot(rows, W[i, 0:256, :])
        qacc[which, 1] += dot(rows, W[i, 256:512, :])

    def multiply_kv(which, i):
        rows = rows_of(which, i)
        both = W[i, 512:640, :]
        kvacc[which, 0] += dot(rows[:, 0:128], both)
        kvacc[which, 1] += dot(rows[:, 128:256], both)

    def multiply(i):
        multiply_q(0, i)
        multiply_kv(0, i)

    for p in range(PARTS):
        spread(zz, p)
    qacc[...] = jnp.zeros_like(qacc)
    kvacc[...] = jnp.zeros_like(kvacc)

    given_start = pl.multiple_of(plane_start(share // 2, 1 - side) + (share % 2) * 512, 512)

    def norm_rows(b):
        rows = pl.ds(pl.multiple_of(b * 16, 16), 16)
        values = hid[rows, :].astype(F32)
        inverse = lax.rsqrt(jnp.mean(values * values, axis=1, keepdims=True) + 1e-05)

        def normed(start):
            columns = pl.ds(start, 512)
            return (hid[rows, columns].astype(F32) * inverse * gain[:, columns]).astype(BF16)

        given[rows, :] = normed(given_start)
        for e in range(8):
            start = pl.multiple_of(plane_start(e // 2, side) + (e % 2) * 512, 512)
            N[0, e, rows, :] = normed(start)

    def quarter(r):
        return pl.ds(pl.multiple_of(r * 64, 64), 64)

    def give(r):
        return remote(given.at[quarter(r)], N.at[1, share, quarter(r)], n_sent.at[0], n_recv.at[share, r], pair)

    def hand(kind, e, r, device):
        ref = N.at[1, e, quarter(r)]
        return remote(ref, ref, n_sent.at[kind], n_recv.at[e, r], device)

    for copy in load_rows:
        copy.wait()

    def norm_step(r, carry):
        def inner(b, inside_carry):
            norm_rows(r * 4 + b)
            return inside_carry

        lax.fori_loop(0, 4, inner, 0)
        return carry

    lax.fori_loop(0, 4, norm_step, 0)

    def spread_given(r, carry):
        give(r).wait_recv()
        hand(1, share, r, to_xr).start()
        hand(2, share, r, to_xl).start()
        hand(3, share, r, to_xo).start()
        hand(4, share, r, sibling).start()
        return carry

    def pass_given(r, carry):
        for xx, device in ((xl, to_xr), (xr, to_xl), (xo, to_xo)):
            e = xx * 2 + c
            hand(1, e, r, device).wait_recv()
            hand(4, e, r, sibling).start()
        return carry

    def wait_given(r, carry):
        for xx in range(NX):
            hand(4, xx * 2 + 1 - c, r, sibling).wait_recv()
        return carry

    def partner_planes(product, first, last):
        def step(n, carry):
            j = plane(n)

            @pl.when(inside(j))
            def _():
                for k in range(NY):
                    product(1, j * NY + k)

            return carry

        lax.fori_loop(first, last, step, 0)

    def gather_step(n, carry):
        for k in range(4):

            @pl.when(n == WORD_STEPS[k])
            def _(k=k):
                pl.semaphore_wait(word.at[k], 1)
                if k < 3:
                    pass_word(k + 1)

        @pl.when(n == PAIR_STEP - 1)
        def _():
            lax.fori_loop(0, 2, spread_given, 0)

        @pl.when(n == PAIR_STEP)
        def _():
            lax.fori_loop(2, 4, spread_given, 0)

        @pl.when(n == SPREAD_STEP)
        def _():
            lax.fori_loop(0, 4, pass_given, 0)

        ja = plane(n)

        @pl.when(jnp.logical_and(inside(ja), n < 2 * PLANES - 1))
        def _():
            i = ja * NY + y
            for p in range(PARTS):
                block(i, p, up, 0).wait_recv()
                spread(ja, p)

        @pl.when(n == 2)
        def _():
            give(0).start()

        @pl.when(n == 2)
        def _():
            give(1).start()

        @pl.when(n == 3)
        def _():
            give(2).start()

        @pl.when(n == 3)
        def _():
            give(3).start()

        jb = plane(n - LAG_B)

        @pl.when(jnp.logical_and(inside(jb), jnp.logical_and(n >= LAG_B, n < 2 * PLANES - 1 + LAG_B)))
        def _():
            i_left, i_right = jb * NY + yl, jb * NY + yr
            for p in range(PARTS):
                block(i_left, p, to_yr, 1).wait_recv()
                if p < PARTS // 2:
                    block(i_left, p, to_yr, 3).start()
                block(i_right, p, to_yl, 2).wait_recv()
                if p >= PARTS // 2:
                    block(i_right, p, to_yl, 3).start()
            multiply(jb * NY + y)
            multiply(i_left)
            multiply(i_right)

        jc = plane(n - LAG_C)

        @pl.when(jnp.logical_and(inside(jc), n >= LAG_C))
        def _():
            i = jc * NY + yo
            for p in range(PARTS):
                block(i, p, to_yr, 3).wait_recv()
            multiply(i)

        @pl.when(n == PARTNER_STEP)
        def _():
            lax.fori_loop(0, 4, wait_given, 0)
            partner_planes(multiply_q, 0, PARTNER_PLANES)
            partner_planes(multiply_kv, 0, PARTNER_PLANES)

        return carry

    lax.fori_loop(1, 2 * PLANES - 1 + LAG_C, gather_step, 0)

    for copy in load_rest:
        copy.wait()

    def gather_sent():
        def chain_sent(j, carry):
            i = j * NY + y

            @pl.when(go_up(j))
            def _():
                sent(W.at[i], ag_send.at[0, i], up).wait_send()

            @pl.when(go_down(j))
            def _():
                sent(W.at[i], ag_send.at[1, i], down).wait_send()

            return carry

        lax.fori_loop(0, PLANES, chain_sent, 0)
        all_blocks, all_halves = W.at[pl.ds(0, PLANES)], W.at[pl.ds(0, PLANES), pl.ds(0, ROWS // 2)]
        sent(all_blocks, ag_sent.at[0], to_yr).wait_send()
        sent(all_blocks, ag_sent.at[1], to_yl).wait_send()
        sent(all_halves, ag_sent.at[2], to_yr).wait_send()
        sent(all_halves, ag_sent.at[3], to_yl).wait_send()
        sent(given, n_sent.at[0], pair).wait_send()
        for kind, device in ((1, to_xr), (2, to_xl), (3, to_xo)):
            sent(given, n_sent.at[kind], device).wait_send()
        sent(N.at[1, pl.ds(0, 4)], n_sent.at[4], sibling).wait_send()

    lane = lax.broadcasted_iota(jnp.int32, (128, 128), 1)

    def pack_kv(which):
        kva, kvb = kvacc[which, 0], kvacc[which, 1]
        low = kva[:128] + pltpu.roll(kvb[:128], 64, 1)
        high = pltpu.roll(kva[128:], 64, 1) + kvb[128:]
        return jnp.where(lane < 64, low, high)

    def ks_copy():
        return remote(ks, kr, q_send.at[0], q_recv.at[0], pair)

    def qs_copy(h):
        return remote(qs.at[h], qr.at[h], q_send.at[1 + h], q_recv.at[1 + h], pair)

    partner_planes(multiply_kv, PARTNER_PLANES, 2 * PLANES - 1)
    ks[...] = pack_kv(1).astype(BF16)
    ks_copy().start()
    partner_planes(multiply_q, PARTNER_PLANES, 2 * PLANES - 1)
    for h in range(2):
        qs[h] = qacc[1, h].astype(BF16)
        qs_copy(h).start()

    kv_mine = pack_kv(0)
    gather_sent()
    ks_copy().wait()
    kv_own = rotate(kv_mine + kr[...].astype(F32), kcos[...], ksin[...])
    kvs[rank] = kv_own.astype(BF16)

    def peer(step):
        if step == 1:
            return rank + 1 - 2 * (rank % 2)
        if step == 2:
            return (rank + 2) % 4
        return 3 - rank

    def kv_copy(step):
        return remote(kvs.at[rank], kvs.at[rank], kv_send.at[step - 1], kv_recv.at[step - 1], group[step])

    for step in (1, 2, 3):
        kv_copy(step).start()
    q_heads = []
    for h in range(2):
        qs_copy(h).wait()
        q_sum = qacc[0, h] + qr[h].astype(F32)
        q_heads.append(rotate(q_sum, cosine[...], sine[...]).astype(BF16))
    for step in (1, 2, 3):
        kv_copy(step).wait()

    def unpack(shift):
        parts = []
        for part in range(2):
            total = jnp.zeros((128, 128), F32)
            for r in range(4):
                piece = kvs[r].astype(F32)
                amount = (32 * r - shift - 64 * part) % 128
                piece = pltpu.roll(piece, amount, 1) if amount else piece
                total = jnp.where(lane // 32 == r, piece, total)
            parts.append(total)
        return jnp.concatenate(parts, axis=0).astype(BF16)

    k_head, v_head = unpack(0), unpack(32)
    row_id = lax.broadcasted_iota(jnp.int32, (SEQ, SEQ), 0)
    col_id = lax.broadcasted_iota(jnp.int32, (SEQ, SEQ), 1)
    causal = row_id >= col_id
    dk = jnp.zeros((SEQ, HD), F32)
    dv = jnp.zeros((SEQ, HD), F32)
    dq_heads = []
    for h in range(2):
        g_head = gc[:, h * HD : (h + 1) * HD]
        scores = jnp.where(causal, dot_rows(q_heads[h], k_head) * SCALE, -1e30)
        weights = jnp.exp(scores - jnp.max(scores, axis=1, keepdims=True))
        probs = weights / jnp.sum(weights, axis=1, keepdims=True)
        grad_probs = dot_rows(g_head, v_head)
        delta = jnp.sum(probs * grad_probs, axis=1, keepdims=True)
        grad_scores = (probs * (grad_probs - delta) * SCALE).astype(BF16)
        dq = dot(grad_scores, k_head)
        dq_heads.append(rotate(dq, cosine[...], -sine[...]).astype(BF16))
        dk = dk + dot_columns(grad_scores, q_heads[h])
        dv = dv + dot_columns(probs.astype(BF16), g_head)

    def pack(r):
        def shifted(value, amount):
            amount = amount % 128
            return pltpu.roll(value, amount, 1) if amount else value

        total = shifted(dk[:128], -32 * r)
        total = jnp.where(lane // 32 == 1, shifted(dv[:128], 32 - 32 * r), total)
        total = jnp.where(lane // 32 == 2, shifted(dk[128:], 64 - 32 * r), total)
        return jnp.where(lane // 32 == 3, shifted(dv[128:], 96 - 32 * r), total)

    for r in range(4):
        dks[r] = pack(r)
    for step in (1, 2, 3):
        dkr[step - 1] = dks[peer(step)].astype(BF16)

    def dk_copy(step):
        return remote(dkr.at[step - 1], dkr.at[step + 2], dk_send.at[step - 1], dk_recv.at[step - 1], group[step])

    for step in (1, 2, 3):
        dk_copy(step).start()

    def ordered(value, core):
        return jnp.concatenate(
            [value[16 * (8 * b + 2 * a + core) : 16 * (8 * b + 2 * a + core) + 16] for a in range(NX) for b in range(2)],
            axis=0,
        )

    def place(ref, value):
        for core in range(2):
            start = pl.multiple_of(jnp.where(c == core, 128, 0), 128)
            ref[pl.ds(start, 128), :] = ordered(value, core)

    def place_kv(which, value):
        turned = pltpu.roll(value, 64, 1)
        first = jnp.concatenate([jnp.where(lane < 64, value, 0.0), jnp.where(lane < 64, turned, 0.0)], axis=0)
        second = jnp.concatenate([jnp.where(lane < 64, 0.0, turned), jnp.where(lane < 64, 0.0, value)], axis=0)
        place(AK.at[which, 0], first.astype(BF16))
        place(AK.at[which, 1], second.astype(BF16))

    def aq_copy():
        return remote(AQ.at[0], AQ.at[1], a_send.at[0], a_recv.at[0], pair)

    def ak_copy():
        return remote(dkvs.at[0], dkvs.at[1], a_send.at[1], a_recv.at[1], pair)

    place(AQ.at[0], jnp.concatenate(dq_heads, axis=1))
    aq_copy().start()

    def weights_q(i):
        return jnp.concatenate([W[i, 0:256, :], W[i, 256:512, :]], axis=1)

    def query_term(j, carry):
        dq = AQ[0]
        for k in range(NY):
            T[j, k] = dot_rows(dq, weights_q(j * NY + k))
        return carry

    lax.fori_loop(0, PLANES, query_term, 0)
    for step in (1, 2, 3):
        dk_copy(step).wait()
    dkv = dks[rank] + dkr[3].astype(F32) + dkr[4].astype(F32) + dkr[5].astype(F32)
    dkv = rotate(dkv, kcos[...], -ksin[...]).astype(BF16)
    dkvs[0] = dkv
    ak_copy().start()
    place_kv(0, dkv.astype(F32))

    def sib_copy(m):
        return remote(sibs.at[m], sibr.at[m], sib_send.at[0], sib_recv.at[m], sibling)

    def x_copy(kind, m):
        x_dst, h, device = ((xo, 0, to_xr), (xo, 1, to_xl), (xr, 1, to_xr), (xl, 0, to_xl), (xr, 0, to_xr), (xl, 1, to_xl))[kind]
        return remote(S.at[m, x_dst, h], xin.at[m, kind], x_send.at[kind], x_recv.at[m, kind], device)

    def far_copy(m, device):
        return remote(zsend.at[m], zin.at[m], z_send.at[0], z_recv.at[m], device)

    def pair_copy(j):
        return remote(ps.at[j], pr.at[j], p_send.at[0], p_recv.at[j], pair)

    def chunk(m):
        partner = jnp.logical_and(m >= 2, m < 6)
        return partner, jnp.where(m < 2, m, jnp.where(m < 6, m - 2, m - 4))

    def term(m):
        partner, j = chunk(m)

        def add_term(which):
            dkv_a, dkv_b = AK[which, 0], AK[which, 1]
            for k in range(NY):
                i = j * NY + k
                both = W[i, 512:640, :]
                base = T[j, k] if which == 0 else dot_rows(AQ[1], weights_q(i))
                value = base + jnp.concatenate([dot_rows(dkv_a, both), dot_rows(dkv_b, both)], axis=1)
                columns = slice((k % 2) * 256, (k % 2) * 256 + 256)
                sibs[m, k // 2, :, columns] = value[:128].astype(BF16)
                own[m, k // 2, :, columns] = value[128:]

        @pl.when(jnp.logical_not(partner))
        def _():
            add_term(0)

        @pl.when(partner)
        def _():
            add_term(1)

        sib_copy(m).start()

    def over_cores(m):
        sib_copy(m).wait_recv()
        for h in range(2):
            for a in range(NX):
                rows = slice(32 * a, 32 * a + 32)
                S[m, a, h] = (own[m, h, rows, :] + sibr[m, h, rows, :].astype(F32)).astype(BF16)

        for kind in (0, 1, 2, 3):
            x_copy(kind, m).start()

    def over_x(m):
        x_copy(0, m).wait_recv()
        S[m, xr, 0] = (S[m, xr, 0].astype(F32) + xin[m, 0].astype(F32)).astype(BF16)
        x_copy(4, m).start()
        x_copy(1, m).wait_recv()
        S[m, xl, 1] = (S[m, xl, 1].astype(F32) + xin[m, 1].astype(F32)).astype(BF16)
        x_copy(5, m).start()

    def send_far(m, totals):
        partner, j = chunk(m)
        for h in range(2):
            fs[m, 0, h] = totals[h][0:16]
            fs[m, 1, h] = totals[h][16:32]
        zsend[m] = fs[m, 1 - zh].astype(BF16)

        @pl.when(jnp.logical_not(partner))
        def _():
            far_copy(m, far).start()

        @pl.when(partner)
        def _():
            far_copy(m, far_pair).start()
            ps[j] = fs[m, zh].astype(BF16)
            pair_copy(j).start()

    def at_owner_x(m):
        for kind in (2, 3, 4, 5):
            x_copy(kind, m).wait_recv()
        totals = [
            S[m, x, 0].astype(F32) + xin[m, 3].astype(F32) + xin[m, 4].astype(F32),
            S[m, x, 1].astype(F32) + xin[m, 2].astype(F32) + xin[m, 5].astype(F32),
        ]
        send_far(m, totals)

    own_rows = pl.ds(pl.multiple_of(tensor * 16, 16), 16)

    def scale_plane(j, which, h, value):
        columns = pl.ds(pl.multiple_of(plane_start(j, which) + h * 512, 512), 512)
        scaled = value * gain[:, columns]
        G[2 * j + which, h] = scaled
        dots[...] += scaled * hid[own_rows, columns].astype(F32)

    def at_owner(m, carry):
        partner, j = chunk(m)
        far_copy(m, far).wait_recv()

        @pl.when(jnp.logical_not(partner))
        def _():
            for h in range(2):
                scale_plane(j, side, h, fs[m, zh, h] + zin[m, h].astype(F32))

        @pl.when(partner)
        def _():
            pair_copy(j).wait_recv()
            for h in range(2):
                scale_plane(j, 1 - side, h, pr[j, h].astype(F32) + zin[m, h].astype(F32))

        return carry

    dots[...] = jnp.zeros_like(dots)

    def sum_step(n, carry):
        @pl.when(n == 2)
        def _():
            aq_copy().wait()
            ak_copy().wait()
            place_kv(1, dkvs[1].astype(F32))

        @pl.when(n < CHUNKS)
        def _():
            term(n)

        @pl.when(jnp.logical_and(n >= 1, n < CHUNKS + 1))
        def _():
            over_cores(n - 1)

        @pl.when(jnp.logical_and(n >= LAG_X, n < CHUNKS + LAG_X))
        def _():
            over_x(n - LAG_X)

        @pl.when(n >= LAG_O)
        def _():
            at_owner_x(n - LAG_O)

        return carry

    lax.fori_loop(0, CHUNKS + LAG_O, sum_step, 0)

    remote(sibs, sibr, sib_send.at[0], sib_recv.at[0], sibling).wait_send()
    for kind in range(6):
        x_dst = (to_xr, to_xl)[kind % 2]
        remote(S.at[:, 0, 0], xin.at[:, 0], x_send.at[kind], x_recv.at[0, 0], x_dst).wait_send()
    lax.fori_loop(0, CHUNKS, at_owner, 0)
    mean_term = jnp.sum(dots[...], axis=1, keepdims=True) * (1.0 / D)
    own_hidden = hid[own_rows, :].astype(F32)
    inverse = lax.rsqrt(jnp.mean(own_hidden * own_hidden, axis=1, keepdims=True) + 1e-05)
    factor = inverse * inverse * mean_term
    for m in range(NZ):
        for h in range(2):
            columns = slice(m * 1024 + h * 512, m * 1024 + h * 512 + 512)
            value = inverse * (G[m, h] - own_hidden[:, columns] * factor)
            out_ref[:, columns] = value.astype(BF16)

    remote(zsend, zin, z_send.at[0], z_recv.at[0], far).wait_send()
    remote(ps, pr, p_send.at[0], p_recv.at[0], pair).wait_send()


def per_device(hidden, norm_gain, w_query, w_key, w_value, grad_context):
    tables = [jnp.asarray(table) for table in rotary_tables()]
    vmem = pl.BlockSpec(memory_space=pltpu.VMEM)
    hbm = pl.BlockSpec(memory_space=pl.ANY)
    dma = pltpu.SemaphoreType.DMA
    return pl.pallas_call(
        kernel,
        out_shape=jax.ShapeDtypeStruct((16, D), BF16),
        in_specs=[hbm] * 10,
        out_specs=vmem,
        scratch_shapes=[
            pltpu.VMEM((SEQ, D), BF16),
            pltpu.VMEM((1, D), F32),
            pltpu.VMEM((2, 32, 256), BF16),
            pltpu.VMEM((SEQ, 256), BF16),
            pltpu.VMEM((SEQ, HD), F32),
            pltpu.VMEM((SEQ, HD), F32),
            pltpu.VMEM((128, 128), F32),
            pltpu.VMEM((128, 128), F32),
            pltpu.VMEM((SLOTS, ROWS, 128), BF16),
            pltpu.VMEM((2, 8, SEQ, 512), BF16),
            pltpu.VMEM((SEQ, 512), BF16),
            pltpu.VMEM((2, 2, SEQ, HD), F32),
            pltpu.VMEM((2, 2, SEQ, HD), F32),
            pltpu.VMEM((2, SEQ, HD), BF16),
            pltpu.VMEM((2, SEQ, HD), BF16),
            pltpu.VMEM((128, 128), BF16),
            pltpu.VMEM((128, 128), BF16),
            pltpu.VMEM((4, 128, 128), BF16),
            pltpu.VMEM((4, 128, 128), F32),
            pltpu.VMEM((6, 128, 128), BF16),
            pltpu.VMEM((2, SEQ, 256), BF16),
            pltpu.VMEM((2, 2, SEQ, 128), BF16),
            pltpu.VMEM((2, 128, 128), BF16),
            pltpu.VMEM((PLANES, NY, SEQ, 256), F32),
            pltpu.VMEM((CHUNKS, 2, 128, 512), BF16),
            pltpu.VMEM((CHUNKS, 2, 128, 512), BF16),
            pltpu.VMEM((CHUNKS, 2, 128, 512), F32),
            pltpu.VMEM((CHUNKS, NX, 2, 32, 512), BF16),
            pltpu.VMEM((CHUNKS, 6, 32, 512), BF16),
            pltpu.VMEM((CHUNKS, 2, 2, 16, 512), F32),
            pltpu.VMEM((CHUNKS, 2, 16, 512), BF16),
            pltpu.VMEM((CHUNKS, 2, 16, 512), BF16),
            pltpu.VMEM((PLANES, 2, 16, 512), BF16),
            pltpu.VMEM((PLANES, 2, 16, 512), BF16),
            pltpu.VMEM((NZ, 2, 16, 512), F32),
            pltpu.VMEM((16, 512), F32),
            pltpu.SemaphoreType.REGULAR((4,)),
            dma((11,)),
            dma((SLOTS, PARTS)),
            dma((2, SLOTS)),
            dma((4,)),
            dma((8, 4)),
            dma((5,)),
            dma((3,)),
            dma((3,)),
            dma((3,)),
            dma((3,)),
            dma((3,)),
            dma((3,)),
            dma((2,)),
            dma((2,)),
            dma((CHUNKS,)),
            dma((1,)),
            dma((CHUNKS, 6)),
            dma((6,)),
            dma((CHUNKS,)),
            dma((1,)),
            dma((PLANES,)),
            dma((1,)),
        ],
        compiler_params=pltpu.CompilerParams(
            collective_id=0, has_side_effects=True, vmem_limit_bytes=60 * 1024 * 1024
        ),
        name="attention_input_grad",
    )(hidden, norm_gain.reshape(1, D), w_query, w_key.T, w_value.T, grad_context, *tables)


def solution(mesh):
    in_specs = (
        P("dp", None),
        P(),
        P("dp", "tensor"),
        P("dp", "tensor"),
        P("dp", "tensor"),
        P("dp", "tensor"),
    )
    out_specs = P(("dp", "tensor"), None)
    return jax.shard_map(
        per_device, mesh=mesh, in_specs=in_specs, out_specs=out_specs, check_vma=False
    )
```
